32 devices in a mesh: rep: 16 (over z, x, core), shard: 2 (over y).
Axes of the slice: x: 2, y: 2, z: 4, core: 2. Of those that a mesh axis runs over, the one named last changes fastest.
Arguments:
- latents: bfloat16 [128, 32, 32, 640], P(('rep', 'shard'))
- cotangent: bfloat16 [128, 32, 32, 640], P(('rep', 'shard')), may hold values from -6 to 6
- gn_gain: float32 [640], replicated, may hold values from 0.1 to 1.9
- gn_bias: float32 [640], replicated, may hold values from -3 to 3
- conv_weight: bfloat16 [5760, 640], P('shard'), may hold values from -0.078125 to 0.078125
- master: float32 [640, 5760], P('rep', 'shard'), may hold values from -6 to 6
- moment_one: float32 [640, 5760], P('rep', 'shard'), may hold values from -6 to 6
- moment_two: float32 [640, 5760], P('rep', 'shard'), may hold values from 0.1 to 10
- departing: int32 [16], replicated, may hold values from 0 to 1, as said below
- partner: int32 [16], replicated, may hold values from 0 to 15, as said below
Outputs:
- conv_out: bfloat16 [128, 32, 32, 640], P(('rep', 'shard'))
- new_master: float32 [16, 2, 40, 5760], P('rep', None, None, 'shard')
- new_first: float32 [16, 2, 40, 5760], P('rep', None, None, 'shard')
- new_second: float32 [16, 2, 40, 5760], P('rep', None, None, 'shard')
The draws below stay inside these ranges and needn't reach their ends.
Inputs may be any that keep to these rules, and one draw needn't show every extreme that they name: Exactly 8 replicas have departing = 1. partner pairs each departing replica with one staying replica and back: partner[partner[r]] = r and departing[partner[r]] = 1 - departing[r]; at least one replica r has partner[r] = (r + 8) mod 16.
All inputs are finite; a program needn't handle non-finite values.
Results may differ from the reference program's by a relative error of at most 0.007.
Values may be sent and summed in bfloat16 or wider, within the bound.
No kernel may reach another device: no remote copies, remote signals or barrier semaphores. Data moves between devices by JAX's collectives and lax.ppermute only.
A program may use at most 192 MiB of HBM per device.

```python
import math
import jax
import jax.numpy as jnp
from jax import lax

CIN = 640
COUT = 640
GROUPS = 32
H = 32
WID = 32
IMG_REP = 8
KIN = 5760
IMAGES = 128
N_REP = 16
N_SHARD = 2


def pairing(key):
    half_count = N_REP // 2
    first_fixed = jax.random.randint(jax.random.fold_in(key, 5), (), 0, N_REP).astype(jnp.int32)
    second_fixed = ((first_fixed + half_count) % N_REP).astype(jnp.int32)
    index_all = jnp.arange(N_REP, dtype=jnp.int32)
    ranks = jax.random.permutation(jax.random.fold_in(key, 7), N_REP).astype(jnp.int32)
    scores = jnp.where(index_all == first_fixed, N_REP, jnp.where(index_all == second_fixed, N_REP + 1, ranks)).astype(jnp.int32)
    order = jnp.argsort(scores, stable=True).astype(jnp.int32)
    first_side = jnp.concatenate([order[:half_count - 1], order[N_REP - 2:N_REP - 1]])
    second_side = jnp.concatenate([order[half_count - 1:N_REP - 2], order[N_REP - 1:]])
    flips = jax.random.randint(jax.random.fold_in(key, 9), (half_count,), 0, 2).astype(jnp.int32)
    leavers = jnp.where(flips == 1, first_side, second_side).astype(jnp.int32)
    stayers = jnp.where(flips == 1, second_side, first_side).astype(jnp.int32)
    leaving = jnp.zeros((N_REP,), jnp.int32).at[leavers].set(1)
    mates = jnp.zeros((N_REP,), jnp.int32).at[leavers].set(stayers)
    mates = mates.at[stayers].set(leavers)
    return (leaving, mates)


def draw_departing(key, part):
    return pairing(key)[0]


def draw_partner(key, part):
    return pairing(key)[1]


def draw_latents(key, part):
    key_a = jax.random.fold_in(key, 11)
    key_b = jax.random.fold_in(key, 12)
    row_scale = 1.0 + 2.0 * jnp.arange(H, dtype=jnp.float32) / (H - 1)
    chan_scale = jax.random.uniform(key_b, (CIN,), jnp.float32, 0.5, 2.0)
    values = jax.random.normal(key_a, (IMAGES, H, WID, CIN), jnp.float32) * row_scale[:, None, None] * chan_scale
    return values.astype(jnp.bfloat16)


def block_scale(rng, dims, cuts, low, top_value):
    def one(position, parts):
        draws = jax.random.uniform(jax.random.fold_in(jax.random.fold_in(rng, 6), position), (parts,), jnp.float32, low / len(cuts), top_value / len(cuts))
        return jnp.repeat(jnp.exp(draws), dims[position] // parts).reshape((-1,) + (1,) * (len(dims) - position - 1))

    factor_of = one(*cuts[0])
    for cut in cuts[1:]:
        factor_of = factor_of * one(*cut)
    return factor_of


def gaussian(rng, extent, scale, most, split=(), held_as=jnp.bfloat16):
    array = scale * jax.random.normal(rng, extent, jnp.float32)
    if split:
        array = array * block_scale(rng, extent, split, -0.22, 0.18)
    return jnp.clip(array, -most, most).astype(held_as)


def setup_inputs(seed: int = 0) -> dict:
    key_of = jax.random.split(jax.random.key(seed), 11)
    return {
        "latents": draw_latents(jax.random.fold_in(key_of[10], 71), 0),
        "cotangent": gaussian(key_of[1], (IMAGES, H, WID, COUT), 1.0, 6.0, ((0, 32),)),
        "gn_gain": jnp.clip(1.0 + 0.18 * jax.random.normal(key_of[2], (CIN,), jnp.float32), 0.1, 1.9),
        "gn_bias": gaussian(key_of[3], (CIN,), 0.5, 3.0, (), jnp.float32),
        "conv_weight": gaussian(key_of[4], (KIN, COUT), KIN ** -0.5, 0.078125, ((0, 2),)),
        "master": gaussian(key_of[5], (COUT, KIN), 1.0, 6.0, ((0, 16), (1, 2)), jnp.float32),
        "moment_one": gaussian(key_of[6], (COUT, KIN), 1.0, 6.0, ((0, 16), (1, 2)), jnp.float32),
        "moment_two": jnp.clip(jnp.exp(math.log(10.0) - 4.6051702 * jax.random.uniform(key_of[7], (COUT, KIN), jnp.float32) ** block_scale(key_of[7], (COUT, KIN), ((0, 16), (1, 2)), -0.2, 0.2)), 0.1, 10.0),
        "departing": draw_departing(jax.random.fold_in(key_of[10], 71), 0),
        "partner": draw_partner(jax.random.fold_in(key_of[10], 71), 0),
    }


beta_one = 0.9
beta_two = 0.999
step_count = 100.0
learn_rate = 0.01
weight_decay = 0.01
adam_eps = 1e-08
norm_eps = 1e-05

def activate(latent_rep, gn_gain, gn_bias):
    float_in = latent_rep.astype(jnp.float32)
    group_width = CIN // GROUPS
    pixel_count = H * WID * group_width
    chan_sums = lax.optimization_barrier(jnp.sum(float_in, axis=(1, 2)))
    group_mean = chan_sums.reshape(-1, GROUPS, group_width).sum(-1) / pixel_count
    centred = float_in - jnp.repeat(group_mean, group_width, axis=1)[:, None, None, :]
    squares = lax.optimization_barrier(jnp.sum(centred * centred, axis=(1, 2))).reshape(-1, GROUPS, group_width).sum(-1)
    variance = squares / pixel_count
    inverse = jnp.repeat(lax.rsqrt(variance + norm_eps), group_width, axis=1)[:, None, None, :]
    return jax.nn.silu(centred * inverse * gn_gain + gn_bias).astype(jnp.bfloat16)

def gather_taps(padded, row_count, col_count):
    taps = [padded[:, row_off:row_off + row_count, col_off:col_off + col_count, :] for row_off in range(3) for col_off in range(3)]
    return jnp.concatenate(taps, axis=3)

def adam(master, first_moment, second_moment, gradient):
    first_moment = beta_one * first_moment + (1.0 - beta_one) * gradient
    second_moment = beta_two * second_moment + (1.0 - beta_two) * gradient * gradient
    first_hat = first_moment / (1.0 - beta_one ** step_count)
    second_hat = second_moment / (1.0 - beta_two ** step_count)
    master = master - learn_rate * (first_hat / (jnp.sqrt(second_hat) + adam_eps) + weight_decay * master)
    return (master, first_moment, second_moment)

def reference(latents, cotangent, gn_gain, gn_bias, conv_weight, master, moment_one, moment_two, departing, partner):
    img_dev = IMG_REP // N_SHARD
    weight_f = conv_weight.astype(jnp.float32)
    latent_reps = latents.reshape(N_REP, IMG_REP, H, WID, CIN)
    cot_reps = cotangent.reshape(N_REP, IMG_REP, H, WID, COUT)
    staying = (1 - departing).astype(jnp.float32)

    def replica(summed, inputs):
        latent_rep, cot_rep, stay_rep = inputs
        activated = activate(latent_rep, gn_gain, gn_bias)
        padded = jnp.pad(activated, ((0, 0), (1, 1), (1, 1), (0, 0)))
        patches = gather_taps(padded, H, WID).astype(jnp.float32)
        conv_rep = jnp.einsum('ihwk,kc->ihwc', patches, weight_f).astype(jnp.bfloat16)
        blocks = patches.reshape(N_SHARD, img_dev * H * WID, 9 * CIN)
        cot_blocks = cot_rep.astype(jnp.float32).reshape(N_SHARD, img_dev * H * WID, COUT)
        partial_value = jnp.einsum('spk,spc->skc', blocks, cot_blocks).astype(jnp.bfloat16)
        partial_value = lax.optimization_barrier(partial_value).astype(jnp.float32)
        return (summed + stay_rep * lax.optimization_barrier(jnp.sum(partial_value, axis=0)), conv_rep)
    summed, conv_out = lax.scan(replica, jnp.zeros((9 * CIN, COUT), jnp.float32), (latent_reps, cot_reps, staying))
    gradient = (summed / (IMG_REP * (N_REP // 2))).T
    next_master, next_first, next_second = adam(master, moment_one, moment_two, gradient)
    block_cols = COUT // N_REP

    def arrange(state):
        blocks = state.reshape(N_REP, block_cols, 9 * CIN)
        paired = jnp.stack([blocks, blocks[partner]], axis=1)
        return paired * staying[:, None, None, None]
    return (conv_out.reshape(IMAGES, H, WID, COUT), arrange(next_master), arrange(next_first), arrange(next_second))
```

```python
import functools

import jax
import jax.numpy as jnp
import numpy as np
from jax import lax
from jax.experimental import pallas as pl
from jax.experimental.pallas import tpu as pltpu
from jax.sharding import PartitionSpec as P

GROUPS = 32
LANES = 128
MIB = 1024 * 1024
VMEM_LIMIT = 58 * MIB

beta_one = 0.9
beta_two = 0.999
step_count = 100.0
learn_rate = 0.01
weight_decay = 0.01
adam_eps = 1e-08
norm_eps = 1e-05
CHUNKS = (16, 8)

BF16 = jnp.bfloat16
F32 = jnp.float32


def adam(master, first_moment, second_moment, gradient):
    first_moment = beta_one * first_moment + (1.0 - beta_one) * gradient
    second_moment = beta_two * second_moment + (1.0 - beta_two) * gradient * gradient
    first_hat = first_moment / (1.0 - beta_one**step_count)
    second_hat = second_moment / (1.0 - beta_two**step_count)
    master = master - learn_rate * (
        first_hat / (jnp.sqrt(second_hat) + adam_eps) + weight_decay * master
    )
    return (master, first_moment, second_moment)


def norm_kernel(lat_ref, gain_ref, bias_ref, member_ref, out_ref, mean_ref, scale_ref):
    images, rows, width, ch = lat_ref.shape
    tiles = ch // LANES
    count = rows * width * (ch // GROUPS)
    image = pl.program_id(0)

    def group_means(totals):
        by_group = jnp.dot(
            jnp.concatenate(totals, axis=0),
            member_ref[...],
            precision=lax.Precision.HIGHEST,
            preferred_element_type=F32,
        )
        back = lax.dot_general(
            by_group,
            member_ref[...],
            (((1,), (1,)), ((), ())),
            precision=lax.Precision.HIGHEST,
            preferred_element_type=F32,
        )
        sums = jnp.sum(back.reshape(images, 8, ch), axis=1)
        return sums * (1.0 / count)

    def fold(value):
        return jnp.sum(value.reshape(width // 8, 8, ch), axis=0)

    @pl.when(image == 0)
    def _():
        zero = jnp.zeros((8, ch), F32)
        totals = []
        for k in range(images):
            def add_row(row, total, k=k):
                return total + fold(lat_ref[k, row].astype(F32))

            totals.append(lax.fori_loop(0, rows, add_row, zero, unroll=8))
        means = group_means(totals)
        mean_ref[0:images, :] = means
        totals = []
        for k in range(images):
            mean = means[k : k + 1]

            def add_square(row, total, k=k, mean=mean):
                centred = lat_ref[k, row].astype(F32) - mean
                return total + fold(centred * centred)

            totals.append(lax.fori_loop(0, rows, add_square, zero, unroll=8))
        scale_ref[0:images, :] = lax.rsqrt(group_means(totals) + norm_eps) * gain_ref[...]

    mean = mean_ref[pl.ds(image, 1), :]
    scale = scale_ref[pl.ds(image, 1), :]
    bias = bias_ref[...]
    column = lax.broadcasted_iota(jnp.int32, (width, ch), 0)

    def write_row(row, carry):
        half = 0.5 * ((lat_ref[image, row].astype(F32) - mean) * scale + bias)
        act = half + half * jnp.tanh(half)
        before = jnp.where(column == 0, 0.0, pltpu.roll(act, 1, 0))
        after = jnp.where(column == width - 1, 0.0, pltpu.roll(act, width - 1, 0))
        start = pl.multiple_of((row + 1) * width, width)
        for shift, value in enumerate((before, act, after)):
            value = value.astype(BF16)
            for tile in range(tiles):
                out_ref[shift * tiles + tile, 0, pl.ds(start, width), :] = value[
                    :, tile * LANES : (tile + 1) * LANES
                ]
        return carry

    lax.fori_loop(0, rows, write_row, 0, unroll=2)
    edge = jnp.zeros((width, LANES), BF16)
    for slab in range(3 * tiles):
        out_ref[slab, 0, 0:width, :] = edge
        out_ref[slab, 0, (rows + 1) * width : (rows + 2) * width, :] = edge


def norm_slabs(latents, gain, bias):
    images, rows, width, ch = latents.shape
    member = np.zeros((ch, LANES), np.float32)
    member[np.arange(ch), np.arange(ch) // (ch // GROUPS)] = 1.0
    slabs, cells = 3 * ch // LANES, (rows + 2) * width
    return pl.pallas_call(
        norm_kernel,
        grid=(images,),
        in_specs=[
            pl.BlockSpec((images, rows, width, ch), lambda i: (0, 0, 0, 0)),
            pl.BlockSpec((1, ch), lambda i: (0, 0)),
            pl.BlockSpec((1, ch), lambda i: (0, 0)),
            pl.BlockSpec((ch, LANES), lambda i: (0, 0)),
        ],
        out_specs=pl.BlockSpec((slabs, 1, cells, LANES), lambda i: (0, i, 0, 0)),
        out_shape=jax.ShapeDtypeStruct((slabs, images, cells, LANES), BF16),
        scratch_shapes=[pltpu.VMEM((-(-images // 8) * 8, ch), F32)] * 2,
        compiler_params=pltpu.CompilerParams(vmem_limit_bytes=VMEM_LIMIT),
        cost_estimate=pl.CostEstimate(
            flops=20 * latents.size, bytes_accessed=8 * latents.size, transcendentals=latents.size
        ),
        name="norm",
    )(latents, gain.reshape(1, ch), bias.reshape(1, ch), jnp.asarray(member))


def weight_grad_kernel(pairs, table, info, cot_ref, *refs):
    slab_refs, out_ref = refs[:-1], refs[-1]
    images, cells, _ = cot_ref.shape
    inner = len(slab_refs) // 2
    quarter = pl.program_id(0) ^ info[0]
    staying = info[1].astype(F32)
    for k in range(inner):
        total = None
        for image in range(images):
            sides = []
            for side in range(2):
                row = table[(2 * side + 1) * pairs + quarter * inner + k]
                start = pl.multiple_of(row, 32)
                sides.append(slab_refs[2 * k + side][0, image, pl.ds(start, cells), :])
            term = lax.dot_general(
                cot_ref[image],
                jnp.concatenate(sides, axis=1),
                (((0,), (0,)), ((), ())),
                preferred_element_type=F32,
            )
            total = term if total is None else total + term
        value = (total * staying).astype(BF16)
        out_ref[k, 0] = value[:, :LANES]
        out_ref[k, 1] = value[:, LANES:]


def weight_grad(slabs, cot, table, info):
    images, cells, out_ch = cot.shape
    pairs = table.shape[0] // 4
    inner = pairs // 8
    padded = slabs.shape[2]

    def slab_of(k, side):
        def index(step, table_ref, info_ref):
            pair = (step ^ info_ref[0]) * inner + k
            return (table_ref[2 * side * pairs + pair], 0, 0, 0)

        return pl.BlockSpec((1, images, padded, LANES), index)

    return pl.pallas_call(
        functools.partial(weight_grad_kernel, pairs),
        grid_spec=pltpu.PrefetchScalarGridSpec(
            num_scalar_prefetch=2,
            grid=(4,),
            in_specs=[pl.BlockSpec((images, cells, out_ch), lambda p, *_: (0, 0, 0))]
            + [slab_of(k, side) for k in range(inner) for side in range(2)],
            out_specs=pl.BlockSpec((inner, 2, out_ch, LANES), lambda p, *_: (p, 0, 0, 0)),
        ),
        out_shape=jax.ShapeDtypeStruct((4 * inner, 2, out_ch, LANES), BF16),
        compiler_params=pltpu.CompilerParams(vmem_limit_bytes=VMEM_LIMIT),
        cost_estimate=pl.CostEstimate(
            flops=2 * 4 * inner * 2 * LANES * images * cells * out_ch,
            bytes_accessed=4 * 4 * inner * images * padded * LANES,
            transcendentals=0,
        ),
        name="weight_grad",
    )(table, info, cot, *([slabs] * (2 * inner)))


def tile_table(first, tiles, shards, cols, ch, width):
    inner_pairs = tiles // 8
    index = np.arange(8 * inner_pairs)
    bits, inner = index // inner_pairs, index % inner_pairs
    p_core, p_shard, p_x = bits >> 2, (bits >> 1) & 1, bits & 1
    per_tap = ch // LANES
    table = []
    for side in range(2):
        tile = first + p_core * (tiles // 2) + p_x * (tiles // 4) + 2 * inner + side
        tile = np.minimum((p_shard * cols) // LANES + tile, 9 * per_tap - 1)
        tap = tile // per_tap
        table += [(tap % 3) * per_tap + tile % per_tap, (tap // 3) * width]
    return jnp.asarray(np.concatenate(table), jnp.int32)


def forward_kernel(place, slab_ref, own_ref, near_ref, far_ref, *refs):
    out_ref, weight, sems = refs[-3:]
    _, _, padded, _ = slab_ref.shape
    _, cells, out_ch = out_ref.shape
    slabs = slab_ref.shape[0]
    width = (padded - cells) // 2
    own_rows, part_rows = own_ref.shape[0], near_ref.shape[0]

    @pl.when(pl.program_id(0) == 0)
    def _():
        copies = [
            pltpu.make_async_copy(
                ref,
                weight.at[pl.ds(pl.multiple_of(place[index], 16), rows)],
                sems.at[index],
            )
            for index, (ref, rows) in enumerate(
                ((own_ref, own_rows), (near_ref, part_rows), (far_ref, part_rows))
            )
        ]
        for copy in copies:
            copy.start()
        for copy in copies:
            copy.wait()

    block = 512
    for start in range(0, cells, block):
        cols = jnp.concatenate(
            [
                slab_ref[slab, 0, start + width * down : start + width * down + block, :]
                for down in range(3)
                for slab in range(slabs)
            ],
            axis=1,
        )
        total = lax.dot_general(
            weight[...], cols, (((0,), (1,)), ((), ())), preferred_element_type=F32
        )
        out_ref[0, start : start + block, :] = total.astype(BF16).T


def forward(slabs, own, near, far, place, width, first, count, earlier=None):
    slab_count, images, padded, _ = slabs.shape
    cells = padded - 2 * width
    out_ch = own.shape[1]
    rows = own.shape[0] + near.shape[0] + far.shape[0]
    extra = () if earlier is None else (earlier,)
    return pl.pallas_call(
        forward_kernel,
        grid_spec=pltpu.PrefetchScalarGridSpec(
            num_scalar_prefetch=1,
            grid=(count,),
            in_specs=[
                pl.BlockSpec((slab_count, 1, padded, LANES), lambda i, *_: (0, i + first, 0, 0)),
                pl.BlockSpec(memory_space=pl.ANY),
                pl.BlockSpec(memory_space=pl.ANY),
                pl.BlockSpec(memory_space=pl.ANY),
            ]
            + [pl.BlockSpec(memory_space=pl.ANY) for _ in extra],
            out_specs=pl.BlockSpec((1, cells, out_ch), lambda i, *_: (i + first, 0, 0)),
            scratch_shapes=[
                pltpu.VMEM((rows, out_ch), BF16),
                pltpu.SemaphoreType.DMA((3,)),
            ],
        ),
        out_shape=jax.ShapeDtypeStruct((images, cells, out_ch), BF16),
        input_output_aliases={5: 0} if extra else {},
        compiler_params=pltpu.CompilerParams(vmem_limit_bytes=VMEM_LIMIT),
        cost_estimate=pl.CostEstimate(
            flops=2 * count * cells * rows * out_ch,
            bytes_accessed=2 * (rows * out_ch + slab_count * count * padded * LANES),
            transcendentals=0,
        ),
        name="forward",
    )(place, slabs, own, near, far, *extra)


def choose_kernel(partner, *refs):
    out_ref = refs[-1]
    reps = out_ref.shape[0]
    at = 0
    for group in range(0, len(refs) - 1, 4):
        total = refs[group][...].astype(F32)
        for ref in refs[group + 1 : group + 4]:
            total = total + ref[...].astype(F32)
        total = total.astype(BF16)
        tiles = total.shape[0]
        for rep in range(reps):
            out_ref[rep, 0, at : at + tiles] = total[:, rep]
        at += tiles
    for rep in range(reps):
        out_ref[rep, 1] = out_ref[partner[rep], 0]


def choose(parts, partner):
    _, reps, rows, lanes = parts[0].shape
    tiles = sum(part.shape[0] for part in parts) // 4
    return pl.pallas_call(
        choose_kernel,
        in_specs=[pl.BlockSpec(memory_space=pltpu.SMEM)]
        + [pl.BlockSpec(memory_space=pltpu.VMEM)] * len(parts),
        out_specs=pl.BlockSpec(memory_space=pltpu.VMEM),
        out_shape=jax.ShapeDtypeStruct((reps, 2, tiles, rows, lanes), BF16),
        compiler_params=pltpu.CompilerParams(vmem_limit_bytes=VMEM_LIMIT),
        name="choose",
    )(partner, *parts)


def update_kernel(source, images, info, grad_ref, master_ref, one_ref, two_ref, mate_ref, *refs):
    outs, grad = refs[:3], refs[3]
    block_rows, cols = master_ref.shape
    high = grad_ref.shape[3]
    staying = info[1].astype(F32)
    odd = info[2] != 0
    skew = info[3]
    for block in range(2):
        for tile, (upper, lower, inner) in enumerate(source):
            span = slice(tile * LANES, (tile + 1) * LANES)
            top = grad_ref[upper, block, inner].astype(F32)
            low = grad_ref[lower, block, inner].astype(F32)
            grad[0:high, span] = top
            grad[high:block_rows, span] = low[2 * high - block_rows : high]
        gradient = jnp.where(odd, grad[:, LANES // 2 : LANES // 2 + cols], grad[:, 0:cols])
        gradient = gradient / images
        if block == 0:
            state = (master_ref[...], one_ref[...], two_ref[...])
        else:
            state = tuple(mate_ref[0, k].astype(F32) for k in range(3))
        for out, value in zip(outs, adam(*state, gradient)):
            out[0, block] = value * staying


def update(received, source, images, master, one, two, mates, info):
    block_rows, cols = master.shape
    out = jax.ShapeDtypeStruct((1, 2, block_rows, cols), F32)
    whole = [pl.BlockSpec(received.shape, lambda i, *_: (0,) * received.ndim)]
    state = [pl.BlockSpec((block_rows, cols), lambda i, *_: (0, 0))] * 3
    return pl.pallas_call(
        functools.partial(lambda info_ref, *refs: update_kernel(source, images, info_ref, *refs)),
        grid_spec=pltpu.PrefetchScalarGridSpec(
            num_scalar_prefetch=1,
            grid=(1,),
            in_specs=whole
            + state
            + [pl.BlockSpec((1, 3, block_rows, cols), lambda i, info_ref: (info_ref[0], 0, 0, 0))],
            out_specs=[pl.BlockSpec((1, 2, block_rows, cols), lambda i, *_: (0, 0, 0, 0))] * 3,
            scratch_shapes=[pltpu.VMEM((block_rows, len(source) * LANES), F32)],
        ),
        out_shape=[out] * 3,
        compiler_params=pltpu.CompilerParams(vmem_limit_bytes=VMEM_LIMIT),
        name="update",
    )(info, received, master, one, two, mates)


def per_device(
    latents,
    cotangent,
    gn_gain,
    gn_bias,
    conv_weight,
    master,
    moment_one,
    moment_two,
    departing,
    partner,
):
    images, rows, width, ch = latents.shape
    reps, shards = lax.axis_size("rep"), lax.axis_size("shard")
    out_ch = conv_weight.shape[1]
    block_rows, cols = master.shape
    rep, shard = lax.axis_index("rep"), lax.axis_index("shard")
    core, col_x, low_z, high_z = rep & 1, (rep >> 1) & 1, (rep >> 2) & 1, rep >> 3
    staying = 1 - departing[rep]

    def swap_rep(value, bits):
        return lax.ppermute(value, "rep", [(i, i ^ bits) for i in range(reps)])

    def swap_shard(value):
        return lax.ppermute(value, "shard", [(0, 1), (1, 0)])

    def swap_both(value, bits):
        pairs = [(i, i ^ (2 * bits + 1)) for i in range(2 * reps)]
        return lax.ppermute(value, ("rep", "shard"), pairs)

    state = jnp.stack([master, moment_one, moment_two]).astype(BF16)
    mates = lax.all_gather(state, "rep", axis=0, tiled=False)

    own_rows = conv_weight.shape[0]
    part_rows = own_rows // 2
    near = swap_shard(lax.dynamic_slice_in_dim(conv_weight, core * part_rows, part_rows, 0))
    far = swap_rep(near, 1)
    missing = (1 - shard) * own_rows
    place = jnp.stack(
        [shard * own_rows, missing + core * part_rows, missing + (1 - core) * part_rows]
    ).astype(jnp.int32)

    slabs = norm_slabs(latents, gn_gain, gn_bias)

    def add(*terms):
        total = terms[0].astype(F32)
        for term in terms[1:]:
            total = total + term.astype(F32)
        return total.astype(BF16)

    cot = cotangent.reshape(images, rows * width, out_ch)
    here = 4 * core + 2 * shard + col_x
    info_send = jnp.stack([here ^ 4, staying]).astype(jnp.int32)
    info_keep = jnp.stack([here, staying]).astype(jnp.int32)
    high = -(-block_rows // 16) * 8
    pieces, source, first_tile, held_before = [], [], 0, 0
    last_tile = -(-cols // LANES)
    for tiles in CHUNKS:
        inner = tiles // 8
        table = tile_table(first_tile, tiles, shards, cols, ch, width)
        other = swap_rep(weight_grad(slabs, cot, table, info_send), 1)
        if first_tile == 0:
            other, far = lax.optimization_barrier((other, far))
        keep = weight_grad(slabs, cot, table, info_keep)
        quarter = [add(keep[k * inner : (k + 1) * inner], other[k * inner : (k + 1) * inner]) for k in range(4)]
        arrived = (swap_both(quarter[3], 2), swap_shard(quarter[2]), swap_rep(quarter[1], 2))
        if first_tile + tiles >= last_tile:
            conv = forward(slabs, conv_weight, near, far, place, width, 0, images // 2)
            arrived, conv = lax.optimization_barrier((arrived, conv))
        plane = add(quarter[0], *arrived)
        plane = plane.reshape(tiles // 4, reps, block_rows, LANES)
        held = tiles // 8

        def part(d_high, d_low):
            start = (held * (low_z ^ d_low), 0, (block_rows - high) * (high_z ^ d_high), 0)
            return lax.dynamic_slice(plane, start, (held, reps, high, LANES))

        pieces += [part(0, 0), swap_rep(part(1, 1), 12), swap_rep(part(1, 0), 8), swap_rep(part(0, 1), 4)]
        for tile in range(tiles):
            at = 4 * ((tile % (tiles // 4)) // held) + 2 * ((tile % (tiles // 2)) // (tiles // 4))
            at += tile // (tiles // 2)
            source.append((at, at + 8, held_before + tile % held))
        first_tile += tiles
        held_before += held
    source = source[:last_tile]
    conv = forward(slabs, conv_weight, near, far, place, width, images // 2, images - images // 2, conv)
    pieces, conv = lax.optimization_barrier((pieces, conv))
    received = lax.all_to_all(choose(pieces, partner), "rep", 0, 0, tiled=True)

    info = jnp.stack([partner[rep], staying, shard, jnp.zeros_like(shard)]).astype(jnp.int32)
    count = images * shards * (reps // 2)
    new = update(received, source, count, master, moment_one, moment_two, mates, info)
    return (conv.reshape(images, rows, width, out_ch), *new)


def gather_taps(padded, row_count, col_count):
    taps = [
        padded[:, row_off : row_off + row_count, col_off : col_off + col_count, :]
        for row_off in range(3)
        for col_off in range(3)
    ]
    return jnp.concatenate(taps, axis=3)


def group_totals(values, image_count, group_width):
    return jnp.sum(values, axis=(1, 2)).reshape(image_count, GROUPS, group_width).sum(-1)


def fold_states(stacked, partner_index):
    running = jnp.zeros_like(stacked)
    pieces_in = lax.all_gather(stacked.astype(jnp.bfloat16), "rep", axis=1, tiled=True).astype(
        jnp.float32
    )
    block_cols = running.shape[1]
    row_ids = lax.iota(jnp.int32, pieces_in.shape[1])
    slot_ids = lax.iota(jnp.int32, block_cols)
    select = (
        (row_ids[None, :] // block_cols == partner_index)
        & (row_ids[None, :] % block_cols == slot_ids[:, None])
    ).astype(jnp.float32)
    return running + jnp.einsum("br,srk->sbk", select, pieces_in, precision=lax.Precision.HIGHEST)


def per_device_any(
    latents,
    cotangent,
    gn_gain,
    gn_bias,
    conv_weight,
    master,
    moment_one,
    moment_two,
    departing,
    partner,
):
    image_count, row_count, col_count, channels = latents.shape
    group_width = channels // GROUPS
    pixel_count = row_count * col_count * group_width
    float_in = latents.astype(jnp.float32)
    group_mean = group_totals(float_in, image_count, group_width) / pixel_count
    centred = float_in - jnp.repeat(group_mean, group_width, axis=1)[:, None, None, :]
    variance = group_totals(centred * centred, image_count, group_width) / pixel_count
    inverse = jnp.repeat(lax.rsqrt(variance + norm_eps), group_width, axis=1)[:, None, None, :]
    activated = jax.nn.silu(centred * inverse * gn_gain + gn_bias).astype(jnp.bfloat16)
    padded = jnp.pad(activated, ((0, 0), (1, 1), (1, 1), (0, 0)))
    patches = gather_taps(padded, row_count, col_count).reshape(-1, 9 * channels)
    out_cols = conv_weight.shape[1]
    columns = patches
    forward = jnp.dot(
        columns,
        lax.all_gather(conv_weight, "shard", axis=0, tiled=True),
        preferred_element_type=jnp.float32,
    )
    conv_out = forward.astype(jnp.bfloat16).reshape(image_count, row_count, col_count, out_cols)
    cot_flat = cotangent.reshape(-1, cotangent.shape[3])
    columns = patches
    grad_rows = lax.psum_scatter(
        lax.dot_general(
            columns, cot_flat, (((0,), (0,)), ((), ())), preferred_element_type=jnp.float32
        ).astype(jnp.bfloat16),
        "shard",
        scatter_dimension=0,
        tiled=True,
    ).astype(jnp.float32)
    my_index = lax.axis_index("rep")
    staying = (1 - departing[my_index]).astype(jnp.float32)
    partner_index = partner[my_index]
    images = image_count * lax.axis_size("shard") * (lax.axis_size("rep") // 2)
    owned = (
        lax.psum_scatter(
            (grad_rows * staying).astype(jnp.bfloat16), "rep", scatter_dimension=1, tiled=True
        ).astype(jnp.float32)
        / images
    )
    own_state = adam(master, moment_one, moment_two, owned.T)
    received = fold_states(jnp.stack(own_state), partner_index)
    mate_state = (received[0], received[1], received[2])

    def arrange(own_part, mate_part):
        return (jnp.stack([own_part, mate_part]) * staying)[None]

    return (
        conv_out,
        arrange(own_state[0], mate_state[0]),
        arrange(own_state[1], mate_state[1]),
        arrange(own_state[2], mate_state[2]),
    )


def solution(mesh):
    paired = mesh.shape["shard"] == 2 and mesh.shape["rep"] == 16
    return jax.shard_map(
        per_device if paired else per_device_any,
        mesh=mesh,
        in_specs=(
            P(("rep", "shard"), None, None, None),
            P(("rep", "shard"), None, None, None),
            P(),
            P(),
            P("shard", None),
            P("rep", "shard"),
            P("rep", "shard"),
            P("rep", "shard"),
            P(),
            P(),
        ),
        out_specs=(
            P(("rep", "shard"), None, None, None),
            P("rep", None, None, "shard"),
            P("rep", None, None, "shard"),
            P("rep", None, None, "shard"),
        ),
        check_vma=False,
    )
```

```python
import functools

import jax
import jax.numpy as jnp
import numpy as np
from jax import lax
from jax.experimental import pallas as pl
from jax.experimental.pallas import tpu as pltpu
from jax.sharding import PartitionSpec as P

GROUPS = 32
LANES = 128
MIB = 1024 * 1024
VMEM_LIMIT = 58 * MIB
PARTS = 3

beta_one = 0.9
beta_two = 0.999
step_count = 100.0
learn_rate = 0.01
weight_decay = 0.01
adam_eps = 1e-08
norm_eps = 1e-05
CHUNKS = (16, 8)
FORWARD = (2, 0, 1)

BF16 = jnp.bfloat16
F32 = jnp.float32


def adam(master, first_moment, second_moment, gradient):
    first_moment = beta_one * first_moment + (1.0 - beta_one) * gradient
    second_moment = beta_two * second_moment + (1.0 - beta_two) * gradient * gradient
    first_hat = first_moment / (1.0 - beta_one**step_count)
    second_hat = second_moment / (1.0 - beta_two**step_count)
    master = master - learn_rate * (
        first_hat / (jnp.sqrt(second_hat) + adam_eps) + weight_decay * master
    )
    return (master, first_moment, second_moment)


def norm_grad_kernel(
    inners, table, info, departing, lat_ref, gain_ref, bias_ref, member_ref, cot_hbm, slab_hbm, *refs
):
    images, rows, width, ch = lat_ref.shape
    tiles = ch // LANES
    cells = rows * width
    count = cells * (ch // GROUPS)
    halves, (slabs, cot, stage, cot_sem, slab_sems, stage_sems) = refs[:-6], refs[-6:]
    load = pltpu.make_async_copy(cot_hbm, cot, cot_sem)
    load.start()

    def group_means(totals):
        by_group = jnp.dot(
            jnp.concatenate(totals, axis=0),
            member_ref[...],
            precision=lax.Precision.HIGHEST,
            preferred_element_type=F32,
        )
        back = lax.dot_general(
            by_group,
            member_ref[...],
            (((1,), (1,)), ((), ())),
            precision=lax.Precision.HIGHEST,
            preferred_element_type=F32,
        )
        return jnp.sum(back.reshape(images, 8, ch), axis=1) * (1.0 / count)

    def fold(value):
        return jnp.sum(value.reshape(width // 8, 8, ch), axis=0)

    zero = jnp.zeros((8, ch), F32)

    def image_sum(image):
        def add_row(row, total):
            return total + fold(lat_ref[image, row].astype(F32))

        return lax.fori_loop(0, rows, add_row, zero, unroll=8)

    def image_square(image, mean):
        def add_row(row, total):
            centred = lat_ref[image, row].astype(F32) - mean
            return total + fold(centred * centred)

        return lax.fori_loop(0, rows, add_row, zero, unroll=8)

    means = group_means([image_sum(image) for image in range(images)])
    squares = [image_square(image, means[image : image + 1]) for image in range(images)]
    scales = lax.rsqrt(group_means(squares) + norm_eps) * gain_ref[...].reshape(1, ch)
    bias = bias_ref[...].reshape(1, ch)
    column = lax.broadcasted_iota(jnp.int32, (width, ch), 0)
    edge = jnp.zeros((width, LANES), BF16)
    stores = []
    for image in range(images):
        mean, scale = means[image : image + 1], scales[image : image + 1]

        def write_row(row, carry, image=image, mean=mean, scale=scale):
            half = 0.5 * ((lat_ref[image, row].astype(F32) - mean) * scale + bias)
            act = half + half * jnp.tanh(half)
            before = jnp.where(column == 0, 0.0, pltpu.roll(act, 1, 0))
            after = jnp.where(column == width - 1, 0.0, pltpu.roll(act, width - 1, 0))
            start = pl.multiple_of((row + 1) * width, width)
            for shift, value in enumerate((before, act, after)):
                value = value.astype(BF16)
                for tile in range(tiles):
                    slabs[shift * tiles + tile, image, pl.ds(start, width), :] = value[
                        :, tile * LANES : (tile + 1) * LANES
                    ]
            return carry

        for slab in range(3 * tiles):
            slabs[slab, image, 0:width, :] = edge
            slabs[slab, image, cells + width : cells + 2 * width, :] = edge
        lax.fori_loop(0, rows, write_row, 0, unroll=2)
        stores.append(pltpu.make_async_copy(slabs.at[:, image], slab_hbm.at[:, image], slab_sems.at[image]))
        stores[-1].start()

    load.wait()
    here = info[0]
    staying = (1 - departing[info[1]]).astype(F32)
    first = 0
    all_pairs = table.shape[0] // 4
    for chunk, inner in enumerate(inners):
        send_hbm, keep_hbm = halves[2 * chunk : 2 * chunk + 2]

        def finish(slot, keep_hbm=keep_hbm):
            pltpu.make_async_copy(stage.at[slot], keep_hbm.at[0], stage_sems.at[slot]).wait()

        def step(index, carry, first=first, inner=inner, send_hbm=send_hbm, keep_hbm=keep_hbm, finish=finish):
            slot = index % 2

            @pl.when(index >= 2)
            def _():
                finish(slot)

            total = None
            for image in range(images):
                sides = []
                for side in range(2):
                    at = 2 * side * all_pairs + first + index
                    row = pl.multiple_of(table[at + all_pairs], 32)
                    sides.append(slabs[table[at], image, pl.ds(row, cells), :])
                term = lax.dot_general(
                    cot[image],
                    jnp.concatenate(sides, axis=1),
                    (((0,), (0,)), ((), ())),
                    preferred_element_type=F32,
                )
                total = term if total is None else total + term
            value = (total * staying).astype(BF16)
            stage[slot, 0] = value[:, :LANES]
            stage[slot, 1] = value[:, LANES:]
            place = (index // inner) ^ here
            at = (place & 3) * inner + index % inner

            @pl.when(place >= 4)
            def _():
                pltpu.make_async_copy(stage.at[slot], send_hbm.at[at], stage_sems.at[slot]).start()

            @pl.when(place < 4)
            def _():
                pltpu.make_async_copy(stage.at[slot], keep_hbm.at[at], stage_sems.at[slot]).start()

            return carry

        lax.fori_loop(0, 8 * inner, step, 0)
        finish(0)
        finish(1)
        first += 8 * inner
    for store in stores:
        store.wait()


def norm_grad(latents, gain, bias, cot, table, info, departing, inners):
    images, rows, width, ch = latents.shape
    _, cells, out_ch = cot.shape
    member = np.zeros((ch, LANES), np.float32)
    member[np.arange(ch), np.arange(ch) // (ch // GROUPS)] = 1.0
    slabs = (3 * ch // LANES, images, (rows + 2) * width, LANES)
    halves = [
        jax.ShapeDtypeStruct((4 * inner, 2, out_ch, LANES), BF16) for inner in inners for _ in range(2)
    ]
    smem, vmem = pl.BlockSpec(memory_space=pltpu.SMEM), pl.BlockSpec(memory_space=pltpu.VMEM)
    anywhere = pl.BlockSpec(memory_space=pl.ANY)
    return pl.pallas_call(
        functools.partial(norm_grad_kernel, inners),
        in_specs=[smem, smem, smem, vmem, vmem, vmem, vmem, anywhere],
        out_specs=[anywhere] * (1 + len(halves)),
        out_shape=[jax.ShapeDtypeStruct(slabs, BF16)] + halves,
        scratch_shapes=[
            pltpu.VMEM(slabs, BF16),
            pltpu.VMEM(cot.shape, BF16),
            pltpu.VMEM((2, 2, out_ch, LANES), BF16),
            pltpu.SemaphoreType.DMA,
            pltpu.SemaphoreType.DMA((images,)),
            pltpu.SemaphoreType.DMA((2,)),
        ],
        compiler_params=pltpu.CompilerParams(vmem_limit_bytes=VMEM_LIMIT),
        cost_estimate=pl.CostEstimate(
            flops=32 * sum(inners) * LANES * images * cells * out_ch,
            bytes_accessed=10 * latents.size,
            transcendentals=latents.size,
        ),
        name="norm_grad",
    )(table, info, departing, latents, gain, bias, jnp.asarray(member), cot)


def tile_table(chunks, shards, cols, ch, width):
    per_tap = ch // LANES
    first, table = 0, [[], [], [], []]
    for tiles in chunks:
        inner_pairs = tiles // 8
        index = np.arange(8 * inner_pairs)
        bits, inner = index // inner_pairs, index % inner_pairs
        p_core, p_shard, p_x = bits >> 2, (bits >> 1) & 1, bits & 1
        for side in range(2):
            tile = first + p_core * (tiles // 2) + p_x * (tiles // 4) + 2 * inner + side
            tile = np.minimum((p_shard * cols) // LANES + tile, 9 * per_tap - 1)
            tap = tile // per_tap
            table[2 * side].append((tap % 3) * per_tap + tile % per_tap)
            table[2 * side + 1].append((tap // 3) * width)
        first += tiles
    return jnp.asarray(np.concatenate([np.concatenate(row) for row in table]), jnp.int32)


def forward_kernel(first, count, info, slab_hbm, own_ref, near_ref, far_ref, *refs):
    out_ref, weight, cols_ref, weight_sems, cols_sems = refs[-5:]
    slabs, _, padded, _ = slab_hbm.shape
    _, cells, out_ch = out_ref.shape
    width = (padded - cells) // 2
    step = pl.program_id(0)
    slot = step % 2

    def cols_copy(image, at):
        return pltpu.make_async_copy(slab_hbm.at[:, first + image], cols_ref.at[at], cols_sems.at[at])

    @pl.when(step == 0)
    def _():
        cols_copy(0, 0).start()
        copies = []
        for source, ref in enumerate((own_ref, near_ref, far_ref)):
            rows = ref.shape[0] // PARTS
            for part in range(PARTS):
                place = pl.multiple_of(info[2 + source] + part * rows, 16)
                copies.append(
                    pltpu.make_async_copy(
                        ref.at[pl.ds(part * rows, rows)],
                        weight.at[pl.ds(place, rows)],
                        weight_sems.at[source * PARTS + part],
                    )
                )
        for copy in copies:
            copy.start()
        if count > 1:
            cols_copy(1, 1).start()
        for copy in copies:
            copy.wait()

    cols_copy(0, slot).wait()
    block = 512
    for start in range(0, cells, block):
        cols = jnp.concatenate(
            [
                cols_ref[slot, slab, start + width * down : start + width * down + block, :]
                for down in range(3)
                for slab in range(slabs)
            ],
            axis=1,
        )
        total = lax.dot_general(
            weight[...], cols, (((0,), (1,)), ((), ())), preferred_element_type=F32
        )
        out_ref[0, start : start + block, :] = total.astype(BF16).T
    if count > 2:

        @pl.when(step + 2 < count)
        def _():
            cols_copy(step + 2, slot).start()


def forward(slabs, own, near, far, info, width, first, count, earlier=None):
    slab_count, images, padded, _ = slabs.shape
    cells = padded - 2 * width
    out_ch = own.shape[1]
    rows = own.shape[0] + near.shape[0] + far.shape[0]
    extra = () if earlier is None else (earlier,)
    return pl.pallas_call(
        functools.partial(forward_kernel, first, count),
        grid_spec=pltpu.PrefetchScalarGridSpec(
            num_scalar_prefetch=1,
            grid=(count,),
            in_specs=[pl.BlockSpec(memory_space=pl.ANY)] * (4 + len(extra)),
            out_specs=pl.BlockSpec((1, cells, out_ch), lambda i, *_: (i + first, 0, 0)),
            scratch_shapes=[
                pltpu.VMEM((rows, out_ch), BF16),
                pltpu.VMEM((2, slab_count, padded, LANES), BF16),
                pltpu.SemaphoreType.DMA((3 * PARTS,)),
                pltpu.SemaphoreType.DMA((2,)),
            ],
        ),
        out_shape=jax.ShapeDtypeStruct((images, cells, out_ch), BF16),
        input_output_aliases={5: 0} if extra else {},
        compiler_params=pltpu.CompilerParams(vmem_limit_bytes=VMEM_LIMIT),
        cost_estimate=pl.CostEstimate(
            flops=2 * count * cells * rows * out_ch,
            bytes_accessed=2 * (rows * out_ch + slab_count * count * padded * LANES),
            transcendentals=0,
        ),
        name="forward",
    )(info, slabs, own, near, far, *extra)


def pack_kernel(master_ref, one_ref, two_ref, out_ref):
    parts = [master_ref[...], one_ref[...], two_ref[...]]
    spare = out_ref.shape[0] - 3 * master_ref.shape[0]
    if spare:
        parts.append(jnp.zeros((spare, master_ref.shape[1]), F32))
    out_ref[...] = jnp.concatenate(parts, axis=0).astype(BF16)


def pack(master, one, two, reps):
    rows, cols = master.shape
    padded = -(-3 * rows // (8 * reps)) * 8 * reps
    return pl.pallas_call(
        pack_kernel,
        out_shape=jax.ShapeDtypeStruct((padded, cols), BF16),
        compiler_params=pltpu.CompilerParams(vmem_limit_bytes=VMEM_LIMIT),
        name="pack",
    )(master, one, two)


def route_kernel(partner, in_ref, out_ref):
    for rep in range(out_ref.shape[0]):
        out_ref[rep] = in_ref[partner[rep]]


def route(pieces, partner):
    return pl.pallas_call(
        route_kernel,
        in_specs=[pl.BlockSpec(memory_space=pltpu.SMEM), pl.BlockSpec(memory_space=pltpu.VMEM)],
        out_specs=pl.BlockSpec(memory_space=pltpu.VMEM),
        out_shape=jax.ShapeDtypeStruct(pieces.shape, BF16),
        compiler_params=pltpu.CompilerParams(vmem_limit_bytes=VMEM_LIMIT),
        name="route",
    )(partner, pieces)


def choose_kernel(partner, *refs):
    out_ref = refs[-1]
    reps = out_ref.shape[0]
    at = 0
    for group in range(0, len(refs) - 1, 4):
        total = refs[group][...].astype(F32)
        for ref in refs[group + 1 : group + 4]:
            total = total + ref[...].astype(F32)
        total = total.astype(BF16)
        tiles = total.shape[0]
        for rep in range(reps):
            out_ref[rep, 0, at : at + tiles] = total[:, rep]
        at += tiles
    for rep in range(reps):
        out_ref[rep, 1] = out_ref[partner[rep], 0]


def choose(parts, partner):
    _, reps, rows, lanes = parts[0].shape
    tiles = sum(part.shape[0] for part in parts) // 4
    return pl.pallas_call(
        choose_kernel,
        in_specs=[pl.BlockSpec(memory_space=pltpu.SMEM)]
        + [pl.BlockSpec(memory_space=pltpu.VMEM)] * len(parts),
        out_specs=pl.BlockSpec(memory_space=pltpu.VMEM),
        out_shape=jax.ShapeDtypeStruct((reps, 2, tiles, rows, lanes), BF16),
        compiler_params=pltpu.CompilerParams(vmem_limit_bytes=VMEM_LIMIT),
        name="choose",
    )(partner, *parts)


def update_kernel(source, images, info, departing, grad_ref, master_ref, one_ref, two_ref, mate_ref, *refs):
    outs, grad = refs[:3], refs[3]
    block_rows, cols = master_ref.shape
    high = grad_ref.shape[3]
    staying = (1 - departing[info[1]]).astype(F32)
    odd = info[5] != 0
    mates = mate_ref[...].astype(F32)
    for block in range(2):
        for tile, (upper, lower, inner) in enumerate(source):
            span = slice(tile * LANES, (tile + 1) * LANES)
            top = grad_ref[upper, block, inner].astype(F32)
            low = grad_ref[lower, block, inner].astype(F32)
            grad[0:high, span] = top
            grad[high:block_rows, span] = low[2 * high - block_rows : high]
        gradient = jnp.where(odd, grad[:, LANES // 2 : LANES // 2 + cols], grad[:, 0:cols])
        gradient = gradient / images
        if block == 0:
            state = (master_ref[...], one_ref[...], two_ref[...])
        else:
            state = tuple(mates[k * block_rows : (k + 1) * block_rows] for k in range(3))
        for out, value in zip(outs, adam(*state, gradient)):
            out[0, block] = value * staying


def update(received, source, images, master, one, two, mates, info, departing):
    block_rows, cols = master.shape
    out = jax.ShapeDtypeStruct((1, 2, block_rows, cols), F32)
    whole = [pl.BlockSpec(received.shape, lambda i, *_: (0,) * received.ndim)]
    state = [pl.BlockSpec((block_rows, cols), lambda i, *_: (0, 0))] * 3
    return pl.pallas_call(
        functools.partial(update_kernel, source, images),
        grid_spec=pltpu.PrefetchScalarGridSpec(
            num_scalar_prefetch=2,
            grid=(1,),
            in_specs=whole
            + state
            + [pl.BlockSpec(mates.shape, lambda i, *_: (0, 0))],
            out_specs=[pl.BlockSpec((1, 2, block_rows, cols), lambda i, *_: (0, 0, 0, 0))] * 3,
            scratch_shapes=[pltpu.VMEM((block_rows, len(source) * LANES), F32)],
        ),
        out_shape=[out] * 3,
        compiler_params=pltpu.CompilerParams(vmem_limit_bytes=VMEM_LIMIT),
        name="update",
    )(info, departing, received, master, one, two, mates)


def per_device(
    latents,
    cotangent,
    gn_gain,
    gn_bias,
    conv_weight,
    master,
    moment_one,
    moment_two,
    departing,
    partner,
):
    images, rows, width, ch = latents.shape
    reps, shards = lax.axis_size("rep"), lax.axis_size("shard")
    out_ch = conv_weight.shape[1]
    block_rows, cols = master.shape
    rep, shard = lax.axis_index("rep"), lax.axis_index("shard")
    core, col_x, low_z, high_z = rep & 1, (rep >> 1) & 1, (rep >> 2) & 1, rep >> 3

    def swap_rep(value, bits):
        return lax.ppermute(value, "rep", [(i, i ^ bits) for i in range(reps)])

    def swap_shard(value):
        return lax.ppermute(value, "shard", [(0, 1), (1, 0)])

    def swap_both(value, bits):
        pairs = [(i, i ^ (2 * bits + 1)) for i in range(2 * reps)]
        return lax.ppermute(value, ("rep", "shard"), pairs)

    own_rows = conv_weight.shape[0]
    part_rows = own_rows // 2
    near = swap_shard(lax.dynamic_slice_in_dim(conv_weight, core * part_rows, part_rows, 0))

    here = 4 * core + 2 * shard + col_x
    missing = (1 - shard) * own_rows
    info = jnp.stack(
        [
            here,
            rep,
            shard * own_rows,
            missing + core * part_rows,
            missing + (1 - core) * part_rows,
            shard,
        ]
    ).astype(jnp.int32)

    def add(*terms):
        total = terms[0].astype(F32)
        for term in terms[1:]:
            total = total + term.astype(F32)
        return total.astype(BF16)

    conv, done = None, 0

    def convolve(count):
        nonlocal conv, done
        if count:
            conv = forward(slabs, conv_weight, near, far, info, width, done, count, conv)
            done += count

    state = pack(master, moment_one, moment_two, reps)
    spread = lax.all_to_all(state, "rep", 0, 0, tiled=True)

    cot = cotangent.reshape(images, rows * width, out_ch)
    inners = [tiles // 8 for tiles in CHUNKS]
    table = tile_table(CHUNKS, shards, cols, ch, width)
    slabs, *halves = norm_grad(latents, gn_gain, gn_bias, cot, table, info, departing, inners)
    sends, keeps = halves[0::2], halves[1::2]
    sends, near, spread = lax.optimization_barrier((sends, near, spread))
    far = swap_rep(near, 1)

    others = [swap_rep(send, 1) for send in sends]
    routed = route(spread.reshape(reps, -1, cols), partner)
    mates = lax.all_to_all(routed.reshape(-1, cols), "rep", 0, 0, tiled=True)
    mine, arriving = [], []
    for inner, keep, other in zip(inners, keeps, others):
        if mine:
            other, quarter = lax.optimization_barrier((other, quarter))
            mine[-1] = quarter[0]
        quarter = [add(keep[k * inner : (k + 1) * inner], other[k * inner : (k + 1) * inner]) for k in range(4)]
        mine.append(quarter[0])
        arriving.append((swap_both(quarter[3], 2), swap_shard(quarter[2]), swap_rep(quarter[1], 2)))

    near, far, mine[-1] = lax.optimization_barrier((near, far, mine[-1]))

    high = -(-block_rows // 16) * 8
    pieces, source, held_before = [], [], 0
    for chunk, tiles in enumerate(CHUNKS):
        arrived = arriving[chunk]
        if FORWARD[chunk]:
            convolve(FORWARD[chunk])
            arrived, conv = lax.optimization_barrier((arrived, conv))
        if chunk == 0:
            arrived, mates = lax.optimization_barrier((arrived, mates))
        else:
            arrived, pieces[-1] = lax.optimization_barrier((arrived, pieces[-1]))
        plane = add(mine[chunk], *arrived).reshape(tiles // 4, reps, block_rows, LANES)
        held = tiles // 8

        def part(d_high, d_low):
            start = (held * (low_z ^ d_low), 0, (block_rows - high) * (high_z ^ d_high), 0)
            return lax.dynamic_slice(plane, start, (held, reps, high, LANES))

        pieces += [part(0, 0), swap_rep(part(1, 1), 12), swap_rep(part(1, 0), 8), swap_rep(part(0, 1), 4)]
        for tile in range(tiles):
            at = 4 * ((tile % (tiles // 4)) // held) + 2 * ((tile % (tiles // 2)) // (tiles // 4))
            at += tile // (tiles // 2)
            source.append((at, at + 8, held_before + tile % held))
        held_before += held
    source = source[: -(-cols // LANES)]
    if FORWARD[-1]:
        convolve(FORWARD[-1])
        pieces, conv = lax.optimization_barrier((pieces, conv))
    received = lax.all_to_all(choose(pieces, partner), "rep", 0, 0, tiled=True)
    if done < images:
        convolve(images - done)
        received, conv = lax.optimization_barrier((received, conv))
    count = images * shards * (reps // 2)
    new = update(received, source, count, master, moment_one, moment_two, mates, info, departing)
    return (conv.reshape(images, rows, width, out_ch), *new)


def gather_taps(padded, row_count, col_count):
    taps = [
        padded[:, row_off : row_off + row_count, col_off : col_off + col_count, :]
        for row_off in range(3)
        for col_off in range(3)
    ]
    return jnp.concatenate(taps, axis=3)


def group_totals(values, image_count, group_width):
    return jnp.sum(values, axis=(1, 2)).reshape(image_count, GROUPS, group_width).sum(-1)


def fold_states(stacked, partner_index):
    running = jnp.zeros_like(stacked)
    pieces_in = lax.all_gather(stacked.astype(jnp.bfloat16), "rep", axis=1, tiled=True).astype(
        jnp.float32
    )
    block_cols = running.shape[1]
    row_ids = lax.iota(jnp.int32, pieces_in.shape[1])
    slot_ids = lax.iota(jnp.int32, block_cols)
    select = (
        (row_ids[None, :] // block_cols == partner_index)
        & (row_ids[None, :] % block_cols == slot_ids[:, None])
    ).astype(jnp.float32)
    return running + jnp.einsum("br,srk->sbk", select, pieces_in, precision=lax.Precision.HIGHEST)


def per_device_any(
    latents,
    cotangent,
    gn_gain,
    gn_bias,
    conv_weight,
    master,
    moment_one,
    moment_two,
    departing,
    partner,
):
    image_count, row_count, col_count, channels = latents.shape
    group_width = channels // GROUPS
    pixel_count = row_count * col_count * group_width
    float_in = latents.astype(jnp.float32)
    group_mean = group_totals(float_in, image_count, group_width) / pixel_count
    centred = float_in - jnp.repeat(group_mean, group_width, axis=1)[:, None, None, :]
    variance = group_totals(centred * centred, image_count, group_width) / pixel_count
    inverse = jnp.repeat(lax.rsqrt(variance + norm_eps), group_width, axis=1)[:, None, None, :]
    activated = jax.nn.silu(centred * inverse * gn_gain + gn_bias).astype(jnp.bfloat16)
    padded = jnp.pad(activated, ((0, 0), (1, 1), (1, 1), (0, 0)))
    patches = gather_taps(padded, row_count, col_count).reshape(-1, 9 * channels)
    out_cols = conv_weight.shape[1]
    columns = patches
    forward = jnp.dot(
        columns,
        lax.all_gather(conv_weight, "shard", axis=0, tiled=True),
        preferred_element_type=jnp.float32,
    )
    conv_out = forward.astype(jnp.bfloat16).reshape(image_count, row_count, col_count, out_cols)
    cot_flat = cotangent.reshape(-1, cotangent.shape[3])
    columns = patches
    grad_rows = lax.psum_scatter(
        lax.dot_general(
            columns, cot_flat, (((0,), (0,)), ((), ())), preferred_element_type=jnp.float32
        ).astype(jnp.bfloat16),
        "shard",
        scatter_dimension=0,
        tiled=True,
    ).astype(jnp.float32)
    my_index = lax.axis_index("rep")
    staying = (1 - departing[my_index]).astype(jnp.float32)
    partner_index = partner[my_index]
    images = image_count * lax.axis_size("shard") * (lax.axis_size("rep") // 2)
    owned = (
        lax.psum_scatter(
            (grad_rows * staying).astype(jnp.bfloat16), "rep", scatter_dimension=1, tiled=True
        ).astype(jnp.float32)
        / images
    )
    own_state = adam(master, moment_one, moment_two, owned.T)
    received = fold_states(jnp.stack(own_state), partner_index)
    mate_state = (received[0], received[1], received[2])

    def arrange(own_part, mate_part):
        return (jnp.stack([own_part, mate_part]) * staying)[None]

    return (
        conv_out,
        arrange(own_state[0], mate_state[0]),
        arrange(own_state[1], mate_state[1]),
        arrange(own_state[2], mate_state[2]),
    )


def solution(mesh):
    paired = mesh.shape["shard"] == 2 and mesh.shape["rep"] == 16
    return jax.shard_map(
        per_device if paired else per_device_any,
        mesh=mesh,
        in_specs=(
            P(("rep", "shard"), None, None, None),
            P(("rep", "shard"), None, None, None),
            P(),
            P(),
            P("shard", None),
            P("rep", "shard"),
            P("rep", "shard"),
            P("rep", "shard"),
            P(),
            P(),
        ),
        out_specs=(
            P(("rep", "shard"), None, None, None),
            P("rep", None, None, "shard"),
            P("rep", None, None, "shard"),
            P("rep", None, None, "shard"),
        ),
        check_vma=False,
    )
```

```python
import functools

import jax
import jax.numpy as jnp
import numpy as np
from jax import lax
from jax.experimental import pallas as pl
from jax.experimental.pallas import tpu as pltpu
from jax.sharding import PartitionSpec as P

GROUPS = 32
LANES = 128
MIB = 1024 * 1024
VMEM_LIMIT = 58 * MIB
SMALL_LIMIT = 20 * MIB
PARTS = 3

beta_one = 0.9
beta_two = 0.999
step_count = 100.0
learn_rate = 0.01
weight_decay = 0.01
adam_eps = 1e-08
norm_eps = 1e-05
CHUNKS = (16, 8)
FORWARD = (2, 0, 1)

BF16 = jnp.bfloat16
F32 = jnp.float32


def adam(master, first_moment, second_moment, gradient):
    first_moment = beta_one * first_moment + (1.0 - beta_one) * gradient
    second_moment = beta_two * second_moment + (1.0 - beta_two) * gradient * gradient
    first_hat = first_moment / (1.0 - beta_one**step_count)
    second_hat = second_moment / (1.0 - beta_two**step_count)
    master = master - learn_rate * (
        first_hat / (jnp.sqrt(second_hat) + adam_eps) + weight_decay * master
    )
    return (master, first_moment, second_moment)


def norm_grad_kernel(
    inners, table, info, departing, lat_hbm, gain_ref, bias_ref, member_ref, cot_hbm, slab_hbm, *refs
):
    images, rows, width, ch = lat_hbm.shape
    tiles = ch // LANES
    cells = rows * width
    count = cells * (ch // GROUPS)
    halves, (lat_ref, slabs, cot, stage, lat_sems, cot_sem, slab_sems, stage_sems) = refs[:-8], refs[-8:]
    arrivals = [
        pltpu.make_async_copy(lat_hbm.at[image], lat_ref.at[image], lat_sems.at[image])
        for image in range(images)
    ]
    for arrival in arrivals:
        arrival.start()
    load = pltpu.make_async_copy(cot_hbm, cot, cot_sem)
    load.start()

    def group_means(totals):
        by_group = jnp.dot(
            jnp.concatenate(totals, axis=0),
            member_ref[...],
            precision=lax.Precision.HIGHEST,
            preferred_element_type=F32,
        )
        back = lax.dot_general(
            by_group,
            member_ref[...],
            (((1,), (1,)), ((), ())),
            precision=lax.Precision.HIGHEST,
            preferred_element_type=F32,
        )
        return jnp.sum(back.reshape(images, 8, ch), axis=1) * (1.0 / count)

    def fold(value):
        return jnp.sum(value.reshape(width // 8, 8, ch), axis=0)

    zero = jnp.zeros((8, ch), F32)

    def image_sum(image):
        arrivals[image].wait()

        def add_row(row, total):
            return total + fold(lat_ref[image, row].astype(F32))

        return lax.fori_loop(0, rows, add_row, zero, unroll=8)

    def image_square(image, mean):
        def add_row(row, total):
            centred = lat_ref[image, row].astype(F32) - mean
            return total + fold(centred * centred)

        return lax.fori_loop(0, rows, add_row, zero, unroll=8)

    means = group_means([image_sum(image) for image in range(images)])
    squares = [image_square(image, means[image : image + 1]) for image in range(images)]
    scales = lax.rsqrt(group_means(squares) + norm_eps) * gain_ref[...].reshape(1, ch)
    bias = bias_ref[...].reshape(1, ch)
    column = lax.broadcasted_iota(jnp.int32, (width, ch), 0)
    edge = jnp.zeros((width, LANES), BF16)
    stores = []
    for image in range(images):
        mean, scale = means[image : image + 1], scales[image : image + 1]

        def write_row(row, carry, image=image, mean=mean, scale=scale):
            half = 0.5 * ((lat_ref[image, row].astype(F32) - mean) * scale + bias)
            act = half + half * jnp.tanh(half)
            before = jnp.where(column == 0, 0.0, pltpu.roll(act, 1, 0))
            after = jnp.where(column == width - 1, 0.0, pltpu.roll(act, width - 1, 0))
            start = pl.multiple_of((row + 1) * width, width)
            for shift, value in enumerate((before, act, after)):
                value = value.astype(BF16)
                for tile in range(tiles):
                    slabs[shift * tiles + tile, image, pl.ds(start, width), :] = value[
                        :, tile * LANES : (tile + 1) * LANES
                    ]
            return carry

        for slab in range(3 * tiles):
            slabs[slab, image, 0:width, :] = edge
            slabs[slab, image, cells + width : cells + 2 * width, :] = edge
        lax.fori_loop(0, rows, write_row, 0, unroll=2)
        stores.append(pltpu.make_async_copy(slabs.at[:, image], slab_hbm.at[:, image], slab_sems.at[image]))
        stores[-1].start()

    load.wait()
    here = info[0]
    staying = (1 - departing[info[1]]).astype(F32)
    first = 0
    all_pairs = table.shape[0] // 4
    for chunk, inner in enumerate(inners):
        send_hbm, keep_hbm = halves[2 * chunk : 2 * chunk + 2]

        def finish(slot, keep_hbm=keep_hbm):
            pltpu.make_async_copy(stage.at[slot], keep_hbm.at[0], stage_sems.at[slot]).wait()

        def step(index, carry, first=first, inner=inner, send_hbm=send_hbm, keep_hbm=keep_hbm, finish=finish):
            slot = index % 2

            @pl.when(index >= 2)
            def _():
                finish(slot)

            total = None
            for image in range(images):
                sides = []
                for side in range(2):
                    at = 2 * side * all_pairs + first + index
                    row = pl.multiple_of(table[at + all_pairs], 32)
                    sides.append(slabs[table[at], image, pl.ds(row, cells), :])
                term = lax.dot_general(
                    cot[image],
                    jnp.concatenate(sides, axis=1),
                    (((0,), (0,)), ((), ())),
                    preferred_element_type=F32,
                )
                total = term if total is None else total + term
            value = (total * staying).astype(BF16)
            stage[slot, 0] = value[:, :LANES]
            stage[slot, 1] = value[:, LANES:]
            place = (index // inner) ^ here
            at = (place & 3) * inner + index % inner

            @pl.when(place >= 4)
            def _():
                pltpu.make_async_copy(stage.at[slot], send_hbm.at[at], stage_sems.at[slot]).start()

            @pl.when(place < 4)
            def _():
                pltpu.make_async_copy(stage.at[slot], keep_hbm.at[at], stage_sems.at[slot]).start()

            return carry

        lax.fori_loop(0, 8 * inner, step, 0)
        finish(0)
        finish(1)
        first += 8 * inner
    for store in stores:
        store.wait()


def norm_grad(latents, gain, bias, cot, table, info, departing, inners):
    images, rows, width, ch = latents.shape
    _, cells, out_ch = cot.shape
    member = np.zeros((ch, LANES), np.float32)
    member[np.arange(ch), np.arange(ch) // (ch // GROUPS)] = 1.0
    slabs = (3 * ch // LANES, images, (rows + 2) * width, LANES)
    halves = [
        jax.ShapeDtypeStruct((4 * inner, 2, out_ch, LANES), BF16) for inner in inners for _ in range(2)
    ]
    smem, vmem = pl.BlockSpec(memory_space=pltpu.SMEM), pl.BlockSpec(memory_space=pltpu.VMEM)
    anywhere = pl.BlockSpec(memory_space=pl.ANY)
    return pl.pallas_call(
        functools.partial(norm_grad_kernel, inners),
        in_specs=[smem, smem, smem, anywhere, vmem, vmem, vmem, anywhere],
        out_specs=[anywhere] * (1 + len(halves)),
        out_shape=[jax.ShapeDtypeStruct(slabs, BF16)] + halves,
        scratch_shapes=[
            pltpu.VMEM(latents.shape, BF16),
            pltpu.VMEM(slabs, BF16),
            pltpu.VMEM(cot.shape, BF16),
            pltpu.VMEM((2, 2, out_ch, LANES), BF16),
            pltpu.SemaphoreType.DMA((images,)),
            pltpu.SemaphoreType.DMA,
            pltpu.SemaphoreType.DMA((images,)),
            pltpu.SemaphoreType.DMA((2,)),
        ],
        compiler_params=pltpu.CompilerParams(vmem_limit_bytes=VMEM_LIMIT),
        cost_estimate=pl.CostEstimate(
            flops=32 * sum(inners) * LANES * images * cells * out_ch,
            bytes_accessed=10 * latents.size,
            transcendentals=latents.size,
        ),
        name="norm_grad",
    )(table, info, departing, latents, gain, bias, jnp.asarray(member), cot)


def tile_table(chunks, shards, cols, ch, width):
    per_tap = ch // LANES
    first, table = 0, [[], [], [], []]
    for tiles in chunks:
        inner_pairs = tiles // 8
        index = np.arange(8 * inner_pairs)
        bits, inner = index // inner_pairs, index % inner_pairs
        p_core, p_shard, p_x = bits >> 2, (bits >> 1) & 1, bits & 1
        for side in range(2):
            tile = first + p_core * (tiles // 2) + p_x * (tiles // 4) + 2 * inner + side
            tile = np.minimum((p_shard * cols) // LANES + tile, 9 * per_tap - 1)
            tap = tile // per_tap
            table[2 * side].append((tap % 3) * per_tap + tile % per_tap)
            table[2 * side + 1].append((tap // 3) * width)
        first += tiles
    return jnp.asarray(np.concatenate([np.concatenate(row) for row in table]), jnp.int32)


def forward_kernel(first, count, info, slab_hbm, own_ref, near_ref, far_ref, *refs):
    out_ref, weight, cols_ref, weight_sems, cols_sems = refs[-5:]
    slabs, _, padded, _ = slab_hbm.shape
    _, cells, out_ch = out_ref.shape
    width = (padded - cells) // 2
    step = pl.program_id(0)
    slot = step % 2

    class cols_copy:
        def __init__(self, image, at):
            share = slabs // PARTS
            self.copies = [
                pltpu.make_async_copy(
                    slab_hbm.at[part * share : (part + 1) * share, first + image],
                    cols_ref.at[at, part * share : (part + 1) * share],
                    cols_sems.at[at, part],
                )
                for part in range(PARTS)
            ]

        def start(self):
            for copy in self.copies:
                copy.start()

        def wait(self):
            for copy in self.copies:
                copy.wait()

    @pl.when(step == 0)
    def _():
        cols_copy(0, 0).start()
        copies = []
        for source, ref in enumerate((own_ref, near_ref, far_ref)):
            rows = ref.shape[0] // PARTS
            for part in range(PARTS):
                place = pl.multiple_of(info[2 + source] + part * rows, 16)
                copies.append(
                    pltpu.make_async_copy(
                        ref.at[pl.ds(part * rows, rows)],
                        weight.at[pl.ds(place, rows)],
                        weight_sems.at[source * PARTS + part],
                    )
                )
        for copy in copies:
            copy.start()
        if count > 1:
            cols_copy(1, 1).start()
        for copy in copies:
            copy.wait()

    cols_copy(0, slot).wait()
    block = 512
    for start in range(0, cells, block):
        cols = jnp.concatenate(
            [
                cols_ref[slot, slab, start + width * down : start + width * down + block, :]
                for down in range(3)
                for slab in range(slabs)
            ],
            axis=1,
        )
        total = lax.dot_general(
            weight[...], cols, (((0,), (1,)), ((), ())), preferred_element_type=F32
        )
        out_ref[0, start : start + block, :] = total.astype(BF16).T
    if count > 2:

        @pl.when(step + 2 < count)
        def _():
            cols_copy(step + 2, slot).start()


def forward(slabs, own, near, far, info, width, first, count, earlier=None):
    slab_count, images, padded, _ = slabs.shape
    cells = padded - 2 * width
    out_ch = own.shape[1]
    rows = own.shape[0] + near.shape[0] + far.shape[0]
    extra = () if earlier is None else (earlier,)
    return pl.pallas_call(
        functools.partial(forward_kernel, first, count),
        grid_spec=pltpu.PrefetchScalarGridSpec(
            num_scalar_prefetch=1,
            grid=(count,),
            in_specs=[pl.BlockSpec(memory_space=pl.ANY)] * (4 + len(extra)),
            out_specs=pl.BlockSpec((1, cells, out_ch), lambda i, *_: (i + first, 0, 0)),
            scratch_shapes=[
                pltpu.VMEM((rows, out_ch), BF16),
                pltpu.VMEM((2, slab_count, padded, LANES), BF16),
                pltpu.SemaphoreType.DMA((3 * PARTS,)),
                pltpu.SemaphoreType.DMA((2, PARTS)),
            ],
        ),
        out_shape=jax.ShapeDtypeStruct((images, cells, out_ch), BF16),
        input_output_aliases={5: 0} if extra else {},
        compiler_params=pltpu.CompilerParams(vmem_limit_bytes=VMEM_LIMIT),
        cost_estimate=pl.CostEstimate(
            flops=2 * count * cells * rows * out_ch,
            bytes_accessed=2 * (rows * out_ch + slab_count * count * padded * LANES),
            transcendentals=0,
        ),
        name="forward",
    )(info, slabs, own, near, far, *extra)


def pack_kernel(master_ref, one_ref, two_ref, out_ref):
    parts = [master_ref[...], one_ref[...], two_ref[...]]
    spare = out_ref.shape[0] - 3 * master_ref.shape[0]
    if spare:
        parts.append(jnp.zeros((spare, master_ref.shape[1]), F32))
    out_ref[...] = jnp.concatenate(parts, axis=0).astype(BF16)


def pack(master, one, two, reps):
    rows, cols = master.shape
    padded = -(-3 * rows // (8 * reps)) * 8 * reps
    return pl.pallas_call(
        pack_kernel,
        out_shape=jax.ShapeDtypeStruct((padded, cols), BF16),
        compiler_params=pltpu.CompilerParams(vmem_limit_bytes=SMALL_LIMIT),
        name="pack",
    )(master, one, two)


def route_kernel(partner, in_ref, out_ref):
    for rep in range(out_ref.shape[0]):
        out_ref[rep] = in_ref[partner[rep]]


def route(pieces, partner):
    return pl.pallas_call(
        route_kernel,
        in_specs=[pl.BlockSpec(memory_space=pltpu.SMEM), pl.BlockSpec(memory_space=pltpu.VMEM)],
        out_specs=pl.BlockSpec(memory_space=pltpu.VMEM),
        out_shape=jax.ShapeDtypeStruct(pieces.shape, BF16),
        compiler_params=pltpu.CompilerParams(vmem_limit_bytes=SMALL_LIMIT),
        name="route",
    )(partner, pieces)


def choose_kernel(partner, *refs):
    out_ref = refs[-1]
    reps = out_ref.shape[0]
    at = 0
    for group in range(0, len(refs) - 1, 4):
        total = refs[group][...].astype(F32)
        for ref in refs[group + 1 : group + 4]:
            total = total + ref[...].astype(F32)
        total = total.astype(BF16)
        tiles = total.shape[0]
        for rep in range(reps):
            out_ref[rep, 0, at : at + tiles] = total[:, rep]
        at += tiles
    for rep in range(reps):
        out_ref[rep, 1] = out_ref[partner[rep], 0]


def choose(parts, partner):
    _, reps, rows, lanes = parts[0].shape
    tiles = sum(part.shape[0] for part in parts) // 4
    return pl.pallas_call(
        choose_kernel,
        in_specs=[pl.BlockSpec(memory_space=pltpu.SMEM)]
        + [pl.BlockSpec(memory_space=pltpu.VMEM)] * len(parts),
        out_specs=pl.BlockSpec(memory_space=pltpu.VMEM),
        out_shape=jax.ShapeDtypeStruct((reps, 2, tiles, rows, lanes), BF16),
        compiler_params=pltpu.CompilerParams(vmem_limit_bytes=SMALL_LIMIT),
        name="choose",
    )(partner, *parts)


def update_kernel(source, images, info, departing, grad_ref, master_ref, one_ref, two_ref, mate_ref, *refs):
    outs, grad = refs[:3], refs[3]
    block_rows, cols = master_ref.shape
    high = grad_ref.shape[3]
    staying = (1 - departing[info[1]]).astype(F32)
    odd = info[5] != 0
    for tile, (upper, lower, inner) in enumerate(source):
        span = slice(tile * LANES, (tile + 1) * LANES)
        grad[0:high, span] = grad_ref[upper, 0, inner].astype(F32)
        low = grad_ref[lower, 0, inner].astype(F32)
        grad[high:block_rows, span] = low[2 * high - block_rows : high]
    gradient = jnp.where(odd, grad[:, LANES // 2 : LANES // 2 + cols], grad[:, 0:cols])
    gradient = gradient / images

    def write(state):
        for out, value in zip(outs, adam(*state, gradient)):
            out[0, 0] = value * staying

    @pl.when(pl.program_id(0) == 0)
    def _():
        write((master_ref[...], one_ref[...], two_ref[...]))

    @pl.when(pl.program_id(0) == 1)
    def _():
        mates = mate_ref[...].astype(F32)
        write(tuple(mates[k * block_rows : (k + 1) * block_rows] for k in range(3)))


def update(received, source, images, master, one, two, mates, info, departing):
    block_rows, cols = master.shape
    out = jax.ShapeDtypeStruct((1, 2, block_rows, cols), F32)
    part = (received.shape[0], 1, *received.shape[2:])
    whole = [pl.BlockSpec(part, lambda i, *_: (0, i, 0, 0, 0))]
    state = [pl.BlockSpec((block_rows, cols), lambda i, *_: (0, 0))] * 3
    return pl.pallas_call(
        functools.partial(update_kernel, source, images),
        grid_spec=pltpu.PrefetchScalarGridSpec(
            num_scalar_prefetch=2,
            grid=(2,),
            in_specs=whole
            + state
            + [pl.BlockSpec(mates.shape, lambda i, *_: (0, 0))],
            out_specs=[pl.BlockSpec((1, 1, block_rows, cols), lambda i, *_: (0, i, 0, 0))] * 3,
            scratch_shapes=[pltpu.VMEM((block_rows, len(source) * LANES), F32)],
        ),
        out_shape=[out] * 3,
        compiler_params=pltpu.CompilerParams(vmem_limit_bytes=SMALL_LIMIT),
        name="update",
    )(info, departing, received, master, one, two, mates)


def per_device(
    latents,
    cotangent,
    gn_gain,
    gn_bias,
    conv_weight,
    master,
    moment_one,
    moment_two,
    departing,
    partner,
):
    images, rows, width, ch = latents.shape
    reps, shards = lax.axis_size("rep"), lax.axis_size("shard")
    out_ch = conv_weight.shape[1]
    block_rows, cols = master.shape
    rep, shard = lax.axis_index("rep"), lax.axis_index("shard")
    core, col_x, low_z, high_z = rep & 1, (rep >> 1) & 1, (rep >> 2) & 1, rep >> 3

    def swap_rep(value, bits):
        return lax.ppermute(value, "rep", [(i, i ^ bits) for i in range(reps)])

    def swap_shard(value):
        return lax.ppermute(value, "shard", [(0, 1), (1, 0)])

    def swap_both(value, bits):
        pairs = [(i, i ^ (2 * bits + 1)) for i in range(2 * reps)]
        return lax.ppermute(value, ("rep", "shard"), pairs)

    own_rows = conv_weight.shape[0]
    part_rows = own_rows // 2
    near = swap_shard(lax.dynamic_slice_in_dim(conv_weight, core * part_rows, part_rows, 0))

    here = 4 * core + 2 * shard + col_x
    missing = (1 - shard) * own_rows
    info = jnp.stack(
        [
            here,
            rep,
            shard * own_rows,
            missing + core * part_rows,
            missing + (1 - core) * part_rows,
            shard,
        ]
    ).astype(jnp.int32)

    def add(*terms):
        total = terms[0].astype(F32)
        for term in terms[1:]:
            total = total + term.astype(F32)
        return total.astype(BF16)

    conv, done = None, 0

    def convolve(count):
        nonlocal conv, done
        if count:
            conv = forward(slabs, conv_weight, near, far, info, width, done, count, conv)
            done += count

    state = pack(master, moment_one, moment_two, reps)
    spread = lax.all_to_all(state, "rep", 0, 0, tiled=True)

    cot = cotangent.reshape(images, rows * width, out_ch)
    inners = [tiles // 8 for tiles in CHUNKS]
    table = tile_table(CHUNKS, shards, cols, ch, width)
    slabs, *halves = norm_grad(latents, gn_gain, gn_bias, cot, table, info, departing, inners)
    sends, keeps = halves[0::2], halves[1::2]
    sends, near, spread = lax.optimization_barrier((sends, near, spread))
    far = swap_rep(near, 1)

    others = [swap_rep(send, 1) for send in sends]
    routed = route(spread.reshape(reps, -1, cols), partner)
    mates = lax.all_to_all(routed.reshape(-1, cols), "rep", 0, 0, tiled=True)
    mine, arriving = [], []
    for inner, keep, other in zip(inners, keeps, others):
        if mine:
            other, quarter = lax.optimization_barrier((other, quarter))
            mine[-1] = quarter[0]
        quarter = [add(keep[k * inner : (k + 1) * inner], other[k * inner : (k + 1) * inner]) for k in range(4)]
        mine.append(quarter[0])
        arriving.append((swap_both(quarter[3], 2), swap_shard(quarter[2]), swap_rep(quarter[1], 2)))

    near, far, mine[-1] = lax.optimization_barrier((near, far, mine[-1]))

    high = -(-block_rows // 16) * 8
    pieces, source, held_before = [], [], 0
    for chunk, tiles in enumerate(CHUNKS):
        arrived = arriving[chunk]
        if FORWARD[chunk]:
            convolve(FORWARD[chunk])
            arrived, conv = lax.optimization_barrier((arrived, conv))
        if chunk == 0:
            arrived, mates = lax.optimization_barrier((arrived, mates))
        else:
            arrived, pieces[-1] = lax.optimization_barrier((arrived, pieces[-1]))
        plane = add(mine[chunk], *arrived).reshape(tiles // 4, reps, block_rows, LANES)
        held = tiles // 8

        def part(d_high, d_low):
            start = (held * (low_z ^ d_low), 0, (block_rows - high) * (high_z ^ d_high), 0)
            return lax.dynamic_slice(plane, start, (held, reps, high, LANES))

        pieces += [part(0, 0), swap_rep(part(1, 1), 12), swap_rep(part(1, 0), 8), swap_rep(part(0, 1), 4)]
        for tile in range(tiles):
            at = 4 * ((tile % (tiles // 4)) // held) + 2 * ((tile % (tiles // 2)) // (tiles // 4))
            at += tile // (tiles // 2)
            source.append((at, at + 8, held_before + tile % held))
        held_before += held
    source = source[: -(-cols // LANES)]
    if FORWARD[-1]:
        convolve(FORWARD[-1])
        pieces, conv = lax.optimization_barrier((pieces, conv))
    received = lax.all_to_all(choose(pieces, partner), "rep", 0, 0, tiled=True)
    if done < images:
        convolve(images - done)
        received, conv = lax.optimization_barrier((received, conv))
    count = images * shards * (reps // 2)
    new = update(received, source, count, master, moment_one, moment_two, mates, info, departing)
    return (conv.reshape(images, rows, width, out_ch), *new)


def gather_taps(padded, row_count, col_count):
    taps = [
        padded[:, row_off : row_off + row_count, col_off : col_off + col_count, :]
        for row_off in range(3)
        for col_off in range(3)
    ]
    return jnp.concatenate(taps, axis=3)


def group_totals(values, image_count, group_width):
    return jnp.sum(values, axis=(1, 2)).reshape(image_count, GROUPS, group_width).sum(-1)


def fold_states(stacked, partner_index):
    running = jnp.zeros_like(stacked)
    pieces_in = lax.all_gather(stacked.astype(jnp.bfloat16), "rep", axis=1, tiled=True).astype(
        jnp.float32
    )
    block_cols = running.shape[1]
    row_ids = lax.iota(jnp.int32, pieces_in.shape[1])
    slot_ids = lax.iota(jnp.int32, block_cols)
    select = (
        (row_ids[None, :] // block_cols == partner_index)
        & (row_ids[None, :] % block_cols == slot_ids[:, None])
    ).astype(jnp.float32)
    return running + jnp.einsum("br,srk->sbk", select, pieces_in, precision=lax.Precision.HIGHEST)


def per_device_any(
    latents,
    cotangent,
    gn_gain,
    gn_bias,
    conv_weight,
    master,
    moment_one,
    moment_two,
    departing,
    partner,
):
    image_count, row_count, col_count, channels = latents.shape
    group_width = channels // GROUPS
    pixel_count = row_count * col_count * group_width
    float_in = latents.astype(jnp.float32)
    group_mean = group_totals(float_in, image_count, group_width) / pixel_count
    centred = float_in - jnp.repeat(group_mean, group_width, axis=1)[:, None, None, :]
    variance = group_totals(centred * centred, image_count, group_width) / pixel_count
    inverse = jnp.repeat(lax.rsqrt(variance + norm_eps), group_width, axis=1)[:, None, None, :]
    activated = jax.nn.silu(centred * inverse * gn_gain + gn_bias).astype(jnp.bfloat16)
    padded = jnp.pad(activated, ((0, 0), (1, 1), (1, 1), (0, 0)))
    patches = gather_taps(padded, row_count, col_count).reshape(-1, 9 * channels)
    out_cols = conv_weight.shape[1]
    columns = patches
    forward = jnp.dot(
        columns,
        lax.all_gather(conv_weight, "shard", axis=0, tiled=True),
        preferred_element_type=jnp.float32,
    )
    conv_out = forward.astype(jnp.bfloat16).reshape(image_count, row_count, col_count, out_cols)
    cot_flat = cotangent.reshape(-1, cotangent.shape[3])
    columns = patches
    grad_rows = lax.psum_scatter(
        lax.dot_general(
            columns, cot_flat, (((0,), (0,)), ((), ())), preferred_element_type=jnp.float32
        ).astype(jnp.bfloat16),
        "shard",
        scatter_dimension=0,
        tiled=True,
    ).astype(jnp.float32)
    my_index = lax.axis_index("rep")
    staying = (1 - departing[my_index]).astype(jnp.float32)
    partner_index = partner[my_index]
    images = image_count * lax.axis_size("shard") * (lax.axis_size("rep") // 2)
    owned = (
        lax.psum_scatter(
            (grad_rows * staying).astype(jnp.bfloat16), "rep", scatter_dimension=1, tiled=True
        ).astype(jnp.float32)
        / images
    )
    own_state = adam(master, moment_one, moment_two, owned.T)
    received = fold_states(jnp.stack(own_state), partner_index)
    mate_state = (received[0], received[1], received[2])

    def arrange(own_part, mate_part):
        return (jnp.stack([own_part, mate_part]) * staying)[None]

    return (
        conv_out,
        arrange(own_state[0], mate_state[0]),
        arrange(own_state[1], mate_state[1]),
        arrange(own_state[2], mate_state[2]),
    )


def solution(mesh):
    paired = mesh.shape["shard"] == 2 and mesh.shape["rep"] == 16
    return jax.shard_map(
        per_device if paired else per_device_any,
        mesh=mesh,
        in_specs=(
            P(("rep", "shard"), None, None, None),
            P(("rep", "shard"), None, None, None),
            P(),
            P(),
            P("shard", None),
            P("rep", "shard"),
            P("rep", "shard"),
            P("rep", "shard"),
            P(),
            P(),
        ),
        out_specs=(
            P(("rep", "shard"), None, None, None),
            P("rep", None, None, "shard"),
            P("rep", None, None, "shard"),
            P("rep", None, None, "shard"),
        ),
        check_vma=False,
    )
```

```python
import functools

import jax
import jax.numpy as jnp
import numpy as np
from jax import lax
from jax.experimental import pallas as pl
from jax.experimental.pallas import tpu as pltpu
from jax.sharding import PartitionSpec as P

GROUPS = 32
LANES = 128
MIB = 1024 * 1024
VMEM_LIMIT = 58 * MIB
SMALL_LIMIT = 20 * MIB
PARTS = 5

beta_one = 0.9
beta_two = 0.999
step_count = 100.0
learn_rate = 0.01
weight_decay = 0.01
adam_eps = 1e-08
norm_eps = 1e-05
CHUNKS = (16, 8)
FORWARD = (2, 0, 1)

BF16 = jnp.bfloat16
F32 = jnp.float32


def adam(master, first_moment, second_moment, gradient):
    first_moment = beta_one * first_moment + (1.0 - beta_one) * gradient
    second_moment = beta_two * second_moment + (1.0 - beta_two) * gradient * gradient
    first_hat = first_moment / (1.0 - beta_one**step_count)
    second_hat = second_moment / (1.0 - beta_two**step_count)
    master = master - learn_rate * (
        first_hat / (jnp.sqrt(second_hat) + adam_eps) + weight_decay * master
    )
    return (master, first_moment, second_moment)


def norm_grad_kernel(
    inners, table, info, departing, lat_hbm, gain_ref, bias_ref, member_ref, cot_hbm, slab_hbm, *refs
):
    images, rows, width, ch = lat_hbm.shape
    tiles = ch // LANES
    cells = rows * width
    count = cells * (ch // GROUPS)
    halves, (lat_ref, slabs, cot, stage, lat_sems, cot_sem, slab_sems, stage_sems) = refs[:-8], refs[-8:]
    arrivals = [
        pltpu.make_async_copy(lat_hbm.at[image], lat_ref.at[image], lat_sems.at[image])
        for image in range(images)
    ]
    for arrival in arrivals:
        arrival.start()
    load = pltpu.make_async_copy(cot_hbm, cot, cot_sem)
    load.start()

    def group_means(totals):
        by_group = jnp.dot(
            jnp.concatenate(totals, axis=0),
            member_ref[...],
            precision=lax.Precision.HIGHEST,
            preferred_element_type=F32,
        )
        back = lax.dot_general(
            by_group,
            member_ref[...],
            (((1,), (1,)), ((), ())),
            precision=lax.Precision.HIGHEST,
            preferred_element_type=F32,
        )
        return jnp.sum(back.reshape(images, 8, ch), axis=1) * (1.0 / count)

    def fold(value):
        return jnp.sum(value.reshape(width // 8, 8, ch), axis=0)

    zero = jnp.zeros((8, ch), F32)

    def image_sum(image):
        arrivals[image].wait()

        def add_row(row, total):
            return total + fold(lat_ref[image, row].astype(F32))

        return lax.fori_loop(0, rows, add_row, zero, unroll=8)

    def image_square(image, mean):
        def add_row(row, total):
            centred = lat_ref[image, row].astype(F32) - mean
            return total + fold(centred * centred)

        return lax.fori_loop(0, rows, add_row, zero, unroll=8)

    means = group_means([image_sum(image) for image in range(images)])
    squares = [image_square(image, means[image : image + 1]) for image in range(images)]
    scales = lax.rsqrt(group_means(squares) + norm_eps) * gain_ref[...].reshape(1, ch)
    bias = bias_ref[...].reshape(1, ch)
    column = lax.broadcasted_iota(jnp.int32, (width, ch), 0)
    edge = jnp.zeros((width, LANES), BF16)
    stores = []
    for image in range(images):
        mean, scale = means[image : image + 1], scales[image : image + 1]

        def write_row(row, carry, image=image, mean=mean, scale=scale):
            half = 0.5 * ((lat_ref[image, row].astype(F32) - mean) * scale + bias)
            act = half + half * jnp.tanh(half)
            before = jnp.where(column == 0, 0.0, pltpu.roll(act, 1, 0))
            after = jnp.where(column == width - 1, 0.0, pltpu.roll(act, width - 1, 0))
            start = pl.multiple_of((row + 1) * width, width)
            for shift, value in enumerate((before, act, after)):
                value = value.astype(BF16)
                for tile in range(tiles):
                    slabs[shift * tiles + tile, image, pl.ds(start, width), :] = value[
                        :, tile * LANES : (tile + 1) * LANES
                    ]
            return carry

        for slab in range(3 * tiles):
            slabs[slab, image, 0:width, :] = edge
            slabs[slab, image, cells + width : cells + 2 * width, :] = edge
        lax.fori_loop(0, rows, write_row, 0)
        stores.append(pltpu.make_async_copy(slabs.at[:, image], slab_hbm.at[:, image], slab_sems.at[image]))
        stores[-1].start()

    load.wait()
    here = info[0]
    staying = (1 - departing[info[1]]).astype(F32)
    first = 0
    all_pairs = table.shape[0] // 4
    for chunk, inner in enumerate(inners):
        send_hbm, keep_hbm = halves[2 * chunk : 2 * chunk + 2]

        def finish(slot, keep_hbm=keep_hbm):
            pltpu.make_async_copy(stage.at[slot], keep_hbm.at[0], stage_sems.at[slot]).wait()

        def step(index, carry, first=first, inner=inner, send_hbm=send_hbm, keep_hbm=keep_hbm, finish=finish):
            slot = index % 2

            @pl.when(index >= 2)
            def _():
                finish(slot)

            total = None
            for image in range(images):
                sides = []
                for side in range(2):
                    at = 2 * side * all_pairs + first + index
                    row = pl.multiple_of(table[at + all_pairs], 32)
                    sides.append(slabs[table[at], image, pl.ds(row, cells), :])
                term = lax.dot_general(
                    cot[image],
                    jnp.concatenate(sides, axis=1),
                    (((0,), (0,)), ((), ())),
                    preferred_element_type=F32,
                )
                total = term if total is None else total + term
            value = (total * staying).astype(BF16)
            stage[slot, 0] = value[:, :LANES]
            stage[slot, 1] = value[:, LANES:]
            place = (index // inner) ^ here
            at = (place & 3) * inner + index % inner

            @pl.when(place >= 4)
            def _():
                pltpu.make_async_copy(stage.at[slot], send_hbm.at[at], stage_sems.at[slot]).start()

            @pl.when(place < 4)
            def _():
                pltpu.make_async_copy(stage.at[slot], keep_hbm.at[at], stage_sems.at[slot]).start()

            return carry

        lax.fori_loop(0, 8 * inner, step, 0)
        finish(0)
        finish(1)
        first += 8 * inner
    for store in stores:
        store.wait()


def norm_grad(latents, gain, bias, cot, table, info, departing, inners):
    images, rows, width, ch = latents.shape
    _, cells, out_ch = cot.shape
    member = np.zeros((ch, LANES), np.float32)
    member[np.arange(ch), np.arange(ch) // (ch // GROUPS)] = 1.0
    slabs = (3 * ch // LANES, images, (rows + 2) * width, LANES)
    halves = [
        jax.ShapeDtypeStruct((4 * inner, 2, out_ch, LANES), BF16) for inner in inners for _ in range(2)
    ]
    smem, vmem = pl.BlockSpec(memory_space=pltpu.SMEM), pl.BlockSpec(memory_space=pltpu.VMEM)
    anywhere = pl.BlockSpec(memory_space=pl.ANY)
    return pl.pallas_call(
        functools.partial(norm_grad_kernel, inners),
        in_specs=[smem, smem, smem, anywhere, vmem, vmem, vmem, anywhere],
        out_specs=[anywhere] * (1 + len(halves)),
        out_shape=[jax.ShapeDtypeStruct(slabs, BF16)] + halves,
        scratch_shapes=[
            pltpu.VMEM(latents.shape, BF16),
            pltpu.VMEM(slabs, BF16),
            pltpu.VMEM(cot.shape, BF16),
            pltpu.VMEM((2, 2, out_ch, LANES), BF16),
            pltpu.SemaphoreType.DMA((images,)),
            pltpu.SemaphoreType.DMA,
            pltpu.SemaphoreType.DMA((images,)),
            pltpu.SemaphoreType.DMA((2,)),
        ],
        compiler_params=pltpu.CompilerParams(vmem_limit_bytes=VMEM_LIMIT),
        cost_estimate=pl.CostEstimate(
            flops=32 * sum(inners) * LANES * images * cells * out_ch,
            bytes_accessed=10 * latents.size,
            transcendentals=latents.size,
        ),
        name="norm_grad",
    )(table, info, departing, latents, gain, bias, jnp.asarray(member), cot)


def tile_table(chunks, shards, cols, ch, width):
    per_tap = ch // LANES
    first, table = 0, [[], [], [], []]
    for tiles in chunks:
        inner_pairs = tiles // 8
        index = np.arange(8 * inner_pairs)
        bits, inner = index // inner_pairs, index % inner_pairs
        p_core, p_shard, p_x = bits >> 2, (bits >> 1) & 1, bits & 1
        for side in range(2):
            tile = first + p_core * (tiles // 2) + p_x * (tiles // 4) + 2 * inner + side
            tile = np.minimum((p_shard * cols) // LANES + tile, 9 * per_tap - 1)
            tap = tile // per_tap
            table[2 * side].append((tap % 3) * per_tap + tile % per_tap)
            table[2 * side + 1].append((tap // 3) * width)
        first += tiles
    return jnp.asarray(np.concatenate([np.concatenate(row) for row in table]), jnp.int32)


def forward_kernel(first, count, info, slab_hbm, own_ref, near_ref, far_ref, *refs):
    out_ref, weight, cols_ref, weight_sems, cols_sems = refs[-5:]
    slabs, _, padded, _ = slab_hbm.shape
    _, cells, out_ch = out_ref.shape
    width = (padded - cells) // 2
    step = pl.program_id(0)
    slot = step % 2

    class cols_copy:
        def __init__(self, image, at):
            share = slabs // PARTS
            self.copies = [
                pltpu.make_async_copy(
                    slab_hbm.at[part * share : (part + 1) * share, first + image],
                    cols_ref.at[at, part * share : (part + 1) * share],
                    cols_sems.at[at, part],
                )
                for part in range(PARTS)
            ]

        def start(self):
            for copy in self.copies:
                copy.start()

        def wait(self):
            for copy in self.copies:
                copy.wait()

    @pl.when(step == 0)
    def _():
        cols_copy(0, 0).start()
        copies = []
        for source, ref in enumerate((own_ref, near_ref, far_ref)):
            rows = ref.shape[0] // PARTS
            for part in range(PARTS):
                place = pl.multiple_of(info[2 + source] + part * rows, 16)
                copies.append(
                    pltpu.make_async_copy(
                        ref.at[pl.ds(part * rows, rows)],
                        weight.at[pl.ds(place, rows)],
                        weight_sems.at[source * PARTS + part],
                    )
                )
        for copy in copies:
            copy.start()
        if count > 1:
            cols_copy(1, 1).start()
        for copy in copies:
            copy.wait()

    cols_copy(0, slot).wait()
    block = 512
    for start in range(0, cells, block):
        cols = jnp.concatenate(
            [
                cols_ref[slot, slab, start + width * down : start + width * down + block, :]
                for down in range(3)
                for slab in range(slabs)
            ],
            axis=1,
        )
        total = lax.dot_general(
            weight[...], cols, (((0,), (1,)), ((), ())), preferred_element_type=F32
        )
        out_ref[0, start : start + block, :] = total.astype(BF16).T
    if count > 2:

        @pl.when(step + 2 < count)
        def _():
            cols_copy(step + 2, slot).start()


def forward(slabs, own, near, far, info, width, first, count, earlier=None):
    slab_count, images, padded, _ = slabs.shape
    cells = padded - 2 * width
    out_ch = own.shape[1]
    rows = own.shape[0] + near.shape[0] + far.shape[0]
    extra = () if earlier is None else (earlier,)
    return pl.pallas_call(
        functools.partial(forward_kernel, first, count),
        grid_spec=pltpu.PrefetchScalarGridSpec(
            num_scalar_prefetch=1,
            grid=(count,),
            in_specs=[pl.BlockSpec(memory_space=pl.ANY)] * (4 + len(extra)),
            out_specs=pl.BlockSpec((1, cells, out_ch), lambda i, *_: (i + first, 0, 0)),
            scratch_shapes=[
                pltpu.VMEM((rows, out_ch), BF16),
                pltpu.VMEM((2, slab_count, padded, LANES), BF16),
                pltpu.SemaphoreType.DMA((3 * PARTS,)),
                pltpu.SemaphoreType.DMA((2, PARTS)),
            ],
        ),
        out_shape=jax.ShapeDtypeStruct((images, cells, out_ch), BF16),
        input_output_aliases={5: 0} if extra else {},
        compiler_params=pltpu.CompilerParams(vmem_limit_bytes=VMEM_LIMIT),
        cost_estimate=pl.CostEstimate(
            flops=2 * count * cells * rows * out_ch,
            bytes_accessed=2 * (rows * out_ch + slab_count * count * padded * LANES),
            transcendentals=0,
        ),
        name="forward",
    )(info, slabs, own, near, far, *extra)


def pack_kernel(master_ref, one_ref, two_ref, out_ref):
    parts = [master_ref[...], one_ref[...], two_ref[...]]
    spare = out_ref.shape[0] - 3 * master_ref.shape[0]
    if spare:
        parts.append(jnp.zeros((spare, master_ref.shape[1]), F32))
    out_ref[...] = jnp.concatenate(parts, axis=0).astype(BF16)


def pack(master, one, two, reps):
    rows, cols = master.shape
    padded = -(-3 * rows // (8 * reps)) * 8 * reps
    return pl.pallas_call(
        pack_kernel,
        out_shape=jax.ShapeDtypeStruct((padded, cols), BF16),
        compiler_params=pltpu.CompilerParams(vmem_limit_bytes=SMALL_LIMIT),
        name="pack",
    )(master, one, two)


def route_kernel(partner, in_ref, out_ref):
    for rep in range(out_ref.shape[0]):
        out_ref[rep] = in_ref[partner[rep]]


def route(pieces, partner):
    return pl.pallas_call(
        route_kernel,
        in_specs=[pl.BlockSpec(memory_space=pltpu.SMEM), pl.BlockSpec(memory_space=pltpu.VMEM)],
        out_specs=pl.BlockSpec(memory_space=pltpu.VMEM),
        out_shape=jax.ShapeDtypeStruct(pieces.shape, BF16),
        compiler_params=pltpu.CompilerParams(vmem_limit_bytes=SMALL_LIMIT),
        name="route",
    )(partner, pieces)


def choose_kernel(partner, *refs):
    out_ref = refs[-1]
    reps = out_ref.shape[0]
    at = 0
    for group in range(0, len(refs) - 1, 4):
        total = refs[group][...].astype(F32)
        for ref in refs[group + 1 : group + 4]:
            total = total + ref[...].astype(F32)
        total = total.astype(BF16)
        tiles = total.shape[0]
        for rep in range(reps):
            out_ref[rep, 0, at : at + tiles] = total[:, rep]
        at += tiles
    for rep in range(reps):
        out_ref[rep, 1] = out_ref[partner[rep], 0]


def choose(parts, partner):
    _, reps, rows, lanes = parts[0].shape
    tiles = sum(part.shape[0] for part in parts) // 4
    return pl.pallas_call(
        choose_kernel,
        in_specs=[pl.BlockSpec(memory_space=pltpu.SMEM)]
        + [pl.BlockSpec(memory_space=pltpu.VMEM)] * len(parts),
        out_specs=pl.BlockSpec(memory_space=pltpu.VMEM),
        out_shape=jax.ShapeDtypeStruct((reps, 2, tiles, rows, lanes), BF16),
        compiler_params=pltpu.CompilerParams(vmem_limit_bytes=SMALL_LIMIT),
        name="choose",
    )(partner, *parts)


def update_kernel(source, images, info, departing, grad_ref, master_ref, one_ref, two_ref, mate_ref, *refs):
    outs, grad = refs[:3], refs[3]
    block_rows, cols = master_ref.shape
    high = grad_ref.shape[3]
    staying = (1 - departing[info[1]]).astype(F32)
    odd = info[5] != 0
    for tile, (upper, lower, inner) in enumerate(source):
        span = slice(tile * LANES, (tile + 1) * LANES)
        grad[0:high, span] = grad_ref[upper, 0, inner].astype(F32)
        low = grad_ref[lower, 0, inner].astype(F32)
        grad[high:block_rows, span] = low[2 * high - block_rows : high]
    gradient = jnp.where(odd, grad[:, LANES // 2 : LANES // 2 + cols], grad[:, 0:cols])
    gradient = gradient / images

    def write(state):
        for out, value in zip(outs, adam(*state, gradient)):
            out[0, 0] = value * staying

    @pl.when(pl.program_id(0) == 0)
    def _():
        write((master_ref[...], one_ref[...], two_ref[...]))

    @pl.when(pl.program_id(0) == 1)
    def _():
        mates = mate_ref[...].astype(F32)
        write(tuple(mates[k * block_rows : (k + 1) * block_rows] for k in range(3)))


def update(received, source, images, master, one, two, mates, info, departing):
    block_rows, cols = master.shape
    out = jax.ShapeDtypeStruct((1, 2, block_rows, cols), F32)
    part = (received.shape[0], 1, *received.shape[2:])
    whole = [pl.BlockSpec(part, lambda i, *_: (0, i, 0, 0, 0))]
    state = [pl.BlockSpec((block_rows, cols), lambda i, *_: (0, 0))] * 3
    return pl.pallas_call(
        functools.partial(update_kernel, source, images),
        grid_spec=pltpu.PrefetchScalarGridSpec(
            num_scalar_prefetch=2,
            grid=(2,),
            in_specs=whole
            + state
            + [pl.BlockSpec(mates.shape, lambda i, *_: (0, 0))],
            out_specs=[pl.BlockSpec((1, 1, block_rows, cols), lambda i, *_: (0, i, 0, 0))] * 3,
            scratch_shapes=[pltpu.VMEM((block_rows, len(source) * LANES), F32)],
        ),
        out_shape=[out] * 3,
        compiler_params=pltpu.CompilerParams(vmem_limit_bytes=SMALL_LIMIT),
        name="update",
    )(info, departing, received, master, one, two, mates)


def per_device(
    latents,
    cotangent,
    gn_gain,
    gn_bias,
    conv_weight,
    master,
    moment_one,
    moment_two,
    departing,
    partner,
):
    images, rows, width, ch = latents.shape
    reps, shards = lax.axis_size("rep"), lax.axis_size("shard")
    out_ch = conv_weight.shape[1]
    block_rows, cols = master.shape
    rep, shard = lax.axis_index("rep"), lax.axis_index("shard")
    core, col_x, low_z, high_z = rep & 1, (rep >> 1) & 1, (rep >> 2) & 1, rep >> 3

    def swap_rep(value, bits):
        return lax.ppermute(value, "rep", [(i, i ^ bits) for i in range(reps)])

    def swap_shard(value):
        return lax.ppermute(value, "shard", [(0, 1), (1, 0)])

    def swap_both(value, bits):
        pairs = [(i, i ^ (2 * bits + 1)) for i in range(2 * reps)]
        return lax.ppermute(value, ("rep", "shard"), pairs)

    own_rows = conv_weight.shape[0]
    part_rows = own_rows // 2
    near = swap_shard(lax.dynamic_slice_in_dim(conv_weight, core * part_rows, part_rows, 0))

    here = 4 * core + 2 * shard + col_x
    missing = (1 - shard) * own_rows
    info = jnp.stack(
        [
            here,
            rep,
            shard * own_rows,
            missing + core * part_rows,
            missing + (1 - core) * part_rows,
            shard,
        ]
    ).astype(jnp.int32)

    def add(*terms):
        total = terms[0].astype(F32)
        for term in terms[1:]:
            total = total + term.astype(F32)
        return total.astype(BF16)

    conv, done = None, 0

    def convolve(count):
        nonlocal conv, done
        if count:
            conv = forward(slabs, conv_weight, near, far, info, width, done, count, conv)
            done += count

    state = pack(master, moment_one, moment_two, reps)
    spread = lax.all_to_all(state, "rep", 0, 0, tiled=True)

    cot = cotangent.reshape(images, rows * width, out_ch)
    inners = [tiles // 8 for tiles in CHUNKS]
    table = tile_table(CHUNKS, shards, cols, ch, width)
    slabs, *halves = norm_grad(latents, gn_gain, gn_bias, cot, table, info, departing, inners)
    sends, keeps = halves[0::2], halves[1::2]
    sends, near, spread = lax.optimization_barrier((sends, near, spread))
    far = swap_rep(near, 1)

    others = [swap_rep(send, 1) for send in sends]
    routed = route(spread.reshape(reps, -1, cols), partner)
    mates = lax.all_to_all(routed.reshape(-1, cols), "rep", 0, 0, tiled=True)
    mine, arriving = [], []
    for inner, keep, other in zip(inners, keeps, others):
        if mine:
            other, quarter = lax.optimization_barrier((other, quarter))
            mine[-1] = quarter[0]
        quarter = [add(keep[k * inner : (k + 1) * inner], other[k * inner : (k + 1) * inner]) for k in range(4)]
        mine.append(quarter[0])
        arriving.append((swap_both(quarter[3], 2), swap_shard(quarter[2]), swap_rep(quarter[1], 2)))

    near, far, mine[-1] = lax.optimization_barrier((near, far, mine[-1]))

    high = -(-block_rows // 16) * 8
    pieces, source, held_before = [], [], 0
    for chunk, tiles in enumerate(CHUNKS):
        arrived = arriving[chunk]
        if FORWARD[chunk]:
            convolve(FORWARD[chunk])
            arrived, conv = lax.optimization_barrier((arrived, conv))
        if chunk == 0:
            arrived, mates = lax.optimization_barrier((arrived, mates))
        else:
            arrived, pieces[-1] = lax.optimization_barrier((arrived, pieces[-1]))
        plane = add(mine[chunk], *arrived).reshape(tiles // 4, reps, block_rows, LANES)
        held = tiles // 8

        def part(d_high, d_low):
            start = (held * (low_z ^ d_low), 0, (block_rows - high) * (high_z ^ d_high), 0)
            return lax.dynamic_slice(plane, start, (held, reps, high, LANES))

        pieces += [part(0, 0), swap_rep(part(1, 1), 12), swap_rep(part(1, 0), 8), swap_rep(part(0, 1), 4)]
        for tile in range(tiles):
            at = 4 * ((tile % (tiles // 4)) // held) + 2 * ((tile % (tiles // 2)) // (tiles // 4))
            at += tile // (tiles // 2)
            source.append((at, at + 8, held_before + tile % held))
        held_before += held
    source = source[: -(-cols // LANES)]
    if FORWARD[-1]:
        convolve(FORWARD[-1])
        pieces, conv = lax.optimization_barrier((pieces, conv))
    received = lax.all_to_all(choose(pieces, partner), "rep", 0, 0, tiled=True)
    if done < images:
        convolve(images - done)
        received, conv = lax.optimization_barrier((received, conv))
    count = images * shards * (reps // 2)
    new = update(received, source, count, master, moment_one, moment_two, mates, info, departing)
    return (conv.reshape(images, rows, width, out_ch), *new)


def gather_taps(padded, row_count, col_count):
    taps = [
        padded[:, row_off : row_off + row_count, col_off : col_off + col_count, :]
        for row_off in range(3)
        for col_off in range(3)
    ]
    return jnp.concatenate(taps, axis=3)


def group_totals(values, image_count, group_width):
    return jnp.sum(values, axis=(1, 2)).reshape(image_count, GROUPS, group_width).sum(-1)


def fold_states(stacked, partner_index):
    running = jnp.zeros_like(stacked)
    pieces_in = lax.all_gather(stacked.astype(jnp.bfloat16), "rep", axis=1, tiled=True).astype(
        jnp.float32
    )
    block_cols = running.shape[1]
    row_ids = lax.iota(jnp.int32, pieces_in.shape[1])
    slot_ids = lax.iota(jnp.int32, block_cols)
    select = (
        (row_ids[None, :] // block_cols == partner_index)
        & (row_ids[None, :] % block_cols == slot_ids[:, None])
    ).astype(jnp.float32)
    return running + jnp.einsum("br,srk->sbk", select, pieces_in, precision=lax.Precision.HIGHEST)


def per_device_any(
    latents,
    cotangent,
    gn_gain,
    gn_bias,
    conv_weight,
    master,
    moment_one,
    moment_two,
    departing,
    partner,
):
    image_count, row_count, col_count, channels = latents.shape
    group_width = channels // GROUPS
    pixel_count = row_count * col_count * group_width
    float_in = latents.astype(jnp.float32)
    group_mean = group_totals(float_in, image_count, group_width) / pixel_count
    centred = float_in - jnp.repeat(group_mean, group_width, axis=1)[:, None, None, :]
    variance = group_totals(centred * centred, image_count, group_width) / pixel_count
    inverse = jnp.repeat(lax.rsqrt(variance + norm_eps), group_width, axis=1)[:, None, None, :]
    activated = jax.nn.silu(centred * inverse * gn_gain + gn_bias).astype(jnp.bfloat16)
    padded = jnp.pad(activated, ((0, 0), (1, 1), (1, 1), (0, 0)))
    patches = gather_taps(padded, row_count, col_count).reshape(-1, 9 * channels)
    out_cols = conv_weight.shape[1]
    columns = patches
    forward = jnp.dot(
        columns,
        lax.all_gather(conv_weight, "shard", axis=0, tiled=True),
        preferred_element_type=jnp.float32,
    )
    conv_out = forward.astype(jnp.bfloat16).reshape(image_count, row_count, col_count, out_cols)
    cot_flat = cotangent.reshape(-1, cotangent.shape[3])
    columns = patches
    grad_rows = lax.psum_scatter(
        lax.dot_general(
            columns, cot_flat, (((0,), (0,)), ((), ())), preferred_element_type=jnp.float32
        ).astype(jnp.bfloat16),
        "shard",
        scatter_dimension=0,
        tiled=True,
    ).astype(jnp.float32)
    my_index = lax.axis_index("rep")
    staying = (1 - departing[my_index]).astype(jnp.float32)
    partner_index = partner[my_index]
    images = image_count * lax.axis_size("shard") * (lax.axis_size("rep") // 2)
    owned = (
        lax.psum_scatter(
            (grad_rows * staying).astype(jnp.bfloat16), "rep", scatter_dimension=1, tiled=True
        ).astype(jnp.float32)
        / images
    )
    own_state = adam(master, moment_one, moment_two, owned.T)
    received = fold_states(jnp.stack(own_state), partner_index)
    mate_state = (received[0], received[1], received[2])

    def arrange(own_part, mate_part):
        return (jnp.stack([own_part, mate_part]) * staying)[None]

    return (
        conv_out,
        arrange(own_state[0], mate_state[0]),
        arrange(own_state[1], mate_state[1]),
        arrange(own_state[2], mate_state[2]),
    )


def solution(mesh):
    paired = mesh.shape["shard"] == 2 and mesh.shape["rep"] == 16
    return jax.shard_map(
        per_device if paired else per_device_any,
        mesh=mesh,
        in_specs=(
            P(("rep", "shard"), None, None, None),
            P(("rep", "shard"), None, None, None),
            P(),
            P(),
            P("shard", None),
            P("rep", "shard"),
            P("rep", "shard"),
            P("rep", "shard"),
            P(),
            P(),
        ),
        out_specs=(
            P(("rep", "shard"), None, None, None),
            P("rep", None, None, "shard"),
            P("rep", None, None, "shard"),
            P("rep", None, None, "shard"),
        ),
        check_vma=False,
    )
```
